128 devices in a mesh: tile: 32 (over x, z, core), grp: 4 (over y).
Axes of the slice: x: 4, y: 4, z: 4, core: 2. Of those that a mesh axis runs over, the one named last changes fastest.
Arguments:
- amplitudes: bfloat16 [2304, 128, 128], P('tile', 'grp'), may hold values from -6 to 6
- ladder_ints: bfloat16 [128, 128, 128, 128], P('grp', None, 'tile'), may hold values from -0.125 to 0.125
- cycle_ints: bfloat16 [48, 128, 48, 128], P(None, 'grp'), may hold values from -0.21875 to 0.21875
- occ_irrep: int32 [48], replicated, may hold values from 0 to 7
- virt_irrep: int32 [128], replicated, may hold values from 0 to 7, as said below
Outputs:
- residual: float32 [48, 48, 128, 128], P(None, 'grp', 'tile')
The draws below stay inside these ranges and needn't reach their ends.
Inputs may be any that keep to these rules, and one draw needn't show every extreme that they name: `occ_irrep`: one of the eight irreducible representations of D2h for each occupied orbital. `virt_irrep`: one of the eight irreducible representations of D2h for each virtual orbital; each irrep labels at most 32 virtual orbitals, and one labels exactly 32.
All inputs are finite; a program needn't handle non-finite values.
Results may differ from the reference program's by a relative error of at most 0.0003.
Values may be sent and summed in bfloat16 or wider, within the bound.
A program may use at most 192 MiB of HBM per device.

```python
import jax
import jax.numpy as jnp
from jax import lax

NO = 48
NV = 128
PAIRS = 2304
VMAX = 32


def draw_virt_irrep(key, part):
    key = jax.random.fold_in(key, 11)
    first_key, second_key, third_key = jax.random.split(key, 3)
    biggest = jax.random.randint(first_key, (), 0, 8)
    slots = jnp.arange(NV, dtype=jnp.int32)
    remain = NV - VMAX
    jitter = jax.random.randint(second_key, (NV,), 0, 2)
    others = jnp.clip(7 * (slots - VMAX) // remain + jitter, 0, 6)
    labels = jnp.where(slots < VMAX, 0, 1 + others)
    labels = (labels + biggest) % 8
    order = jax.random.permutation(third_key, NV)
    return labels[order].astype(jnp.int32)


def set_ends(drawn, stream_key, least, largest):
    extent = drawn.shape
    place = [jax.random.randint(jax.random.fold_in(stream_key, axis), (), 0, extent[axis]) for axis in range(len(extent))]
    drawn = drawn.at[tuple(place)].set(least)
    longest = extent.index(max(extent))
    place[longest] = (place[longest] + 1) % extent[longest]
    return drawn.at[tuple(place)].set(largest)


def block_scale(own_key, shape, cuts, low, high):
    def one(position, shards_of):
        steps = jax.random.uniform(jax.random.fold_in(jax.random.fold_in(own_key, 6), position), (shards_of,), jnp.float32, low / len(cuts), high / len(cuts))
        return jnp.repeat(jnp.exp(steps), shape[position] // shards_of).reshape((-1,) + (1,) * (len(shape) - position - 1))

    loudness = one(*cuts[0])
    for cut in cuts[1:]:
        loudness = loudness * one(*cut)
    return loudness


def normal_values(key, dims, scale, most, shards=(), kind=jnp.bfloat16):
    values = scale * jax.random.normal(key, dims, jnp.float32)
    if shards:
        values = values * block_scale(key, dims, shards, -0.22, 0.18)
    return jnp.clip(values, -most, most).astype(kind)


def setup_inputs(seed: int = 0) -> dict:
    seeds = jax.random.split(jax.random.key(seed), 6)
    amplitudes = normal_values(seeds[0], (PAIRS, NV, NV), 1.0, 6.0, ((0, 32), (1, 4)))
    ladder_ints = normal_values(seeds[1], (NV, NV, NV, NV), (NV * NV // 8) ** -0.5, 0.125, ((0, 4), (2, 32)))
    cycle_ints = normal_values(seeds[2], (NO, NV, NO, NV), (NO * NV // 8) ** -0.5, 0.21875, ((1, 4),))
    occ_irrep = set_ends(jax.random.randint(seeds[3], (NO,), 0, 8), jax.random.fold_in(seeds[3], 1), 0, 7).astype(jnp.int32)
    virt_irrep = draw_virt_irrep(jax.random.fold_in(seeds[5], 71), 0)
    return {"amplitudes": amplitudes, "ladder_ints": ladder_ints, "cycle_ints": cycle_ints, "occ_irrep": occ_irrep, "virt_irrep": virt_irrep}


def reference(amplitudes, ladder_ints, cycle_ints, occ_irrep, virt_irrep):
    pair_irrep = jnp.bitwise_xor(occ_irrep[:, None], occ_irrep[None, :]).reshape(NO * NO)
    virt_pair = jnp.bitwise_xor(virt_irrep[:, None], virt_irrep[None, :])
    allowed = pair_irrep[:, None, None] == virt_pair[None, :, :]
    masked = jnp.where(allowed, amplitudes, jnp.zeros((), jnp.bfloat16))
    flat = masked.reshape(NO * NO, NV * NV)

    def ladder_column(index):
        columns = lax.dynamic_slice_in_dim(ladder_ints, index, 1, 2).reshape(NV * NV, NV)
        return jnp.dot(flat, columns, preferred_element_type=jnp.float32)

    ladder = lax.map(ladder_column, jnp.arange(NV, dtype=jnp.int32))
    ladder = jnp.transpose(ladder, (1, 0, 2)).reshape(NO, NO, NV, NV)
    cycle_left = jnp.transpose(masked.reshape(NO, NO, NV, NV), (0, 3, 1, 2)).reshape(NO * NV, NO * NV)
    cycle_right = cycle_ints.reshape(NO * NV, NO * NV)
    cycle = jnp.dot(cycle_left, cycle_right, preferred_element_type=jnp.float32)
    cycle = jnp.transpose(cycle.reshape(NO, NV, NO, NV), (0, 2, 1, 3))
    combined = 0.5 * ladder + cycle
    flipped = combined - jnp.swapaxes(combined, 2, 3)
    anti = flipped - jnp.swapaxes(flipped, 0, 1)
    return jnp.where(allowed.reshape(NO, NO, NV, NV), anti, jnp.zeros((), jnp.float32))
```

```python
import jax
import jax.numpy as jnp
from jax import lax
from jax.experimental import pallas as pl
from jax.experimental.pallas import tpu as pltpu
from jax.sharding import PartitionSpec as P

NO = 48
NV = 128
SLOTS = 32
PART_C = 32
PART_A = 4
PART_J = 12
TILES = 32
GRPS = 4
ROWS = 72
IRREPS = 8
F32 = jnp.float32
BF16 = jnp.bfloat16
I32 = jnp.int32


def iota(shape, axis):
    return lax.broadcasted_iota(I32, shape, axis)


def lanes_at(values, index):
    return jnp.take_along_axis(values, index, axis=1, mode="promise_in_bounds")


def spread(selector, values):
    return jnp.dot(selector.astype(BF16), values.astype(BF16), preferred_element_type=F32).astype(I32)


def pick_rows(table, which):
    picked = jnp.broadcast_to(table[0:1], which.shape)
    for irrep in range(1, IRREPS):
        picked = jnp.where(which == irrep, jnp.broadcast_to(table[irrep : irrep + 1], which.shape), picked)
    return picked


def column_of(virt_row):
    return jnp.broadcast_to(virt_row, (NV, NV)).astype(F32).T.astype(I32)


def pack_body(occ_s, virt_ref, t_ref, out_ref, table_ref, index_ref, column_ref, rows_ref):
    row = jnp.broadcast_to(virt_ref[...], (NV, NV))
    col = column_of(virt_ref[...])
    column_ref[...] = col
    sub = iota((NV, NV), 0)
    lane = iota((NV, NV), 1)
    same = row == col
    rank_col = jnp.sum(jnp.where(same & (lane < sub), 1.0, 0.0), axis=1, keepdims=True)
    rank_row = jnp.sum(jnp.where(same & (sub < lane), 1.0, 0.0), axis=0, keepdims=True)
    hit = jnp.broadcast_to(rank_col, (NV, NV)).astype(I32) == lane % SLOTS
    subf = sub.astype(F32)
    entries = [
        jnp.sum(jnp.where(hit & (col == irrep), subf, 0.0), axis=0, keepdims=True)
        for irrep in range(IRREPS)
    ]
    table = jnp.concatenate(entries, axis=0).astype(I32)
    table_ref[0:8] = table
    table_ref[8:16] = jnp.broadcast_to(rank_row, (8, NV)).astype(I32)
    c_col = column_ref[pl.ds(pl.multiple_of(lax.axis_index("grp") * PART_C, PART_C), PART_C)]
    for irrep in range(IRREPS):
        index_ref[irrep] = pick_rows(table, c_col ^ irrep)
    first = lax.axis_index("tile") * ROWS
    quarter = iota((8, NV), 1) // SLOTS

    def one_row(r, carry):
        pair = first + r
        irrep = occ_s[pair // NO] ^ occ_s[pair % NO]
        got = lanes_at(t_ref[r].astype(F32), index_ref[irrep])
        row = got[24:32]
        for q in (2, 1, 0):
            row = jnp.where(quarter == q, got[8 * q : 8 * q + 8], row)
        rows_ref[pl.ds(pl.multiple_of(r * 8, 8), 8)] = row
        return carry

    lax.fori_loop(0, ROWS, one_row, 0, unroll=8)
    for block in range(ROWS // 8):
        for half in range(4):
            pair_of = [
                rows_ref[pl.ds(block * 64 + 2 * half + odd, 8, stride=8)] for odd in range(2)
            ]
            out_ref[block, half] = jnp.concatenate(pair_of, axis=0).astype(BF16)


def pack(occ, virt_row, amplitudes):
    return pl.pallas_call(
        pack_body,
        out_shape=(
            jax.ShapeDtypeStruct((ROWS // 8, 4, 16, NV), BF16),
            jax.ShapeDtypeStruct((16, NV), I32),
        ),
        in_specs=[
            pl.BlockSpec(memory_space=pltpu.SMEM),
            pl.BlockSpec(memory_space=pltpu.VMEM),
            pl.BlockSpec(memory_space=pltpu.VMEM),
        ],
        out_specs=(pl.BlockSpec(memory_space=pltpu.VMEM), pl.BlockSpec(memory_space=pltpu.VMEM)),
        scratch_shapes=[
            pltpu.VMEM((IRREPS, PART_C, NV), I32),
            pltpu.VMEM((NV, NV), I32),
            pltpu.VMEM((ROWS * 8, NV), F32),
        ],
        compiler_params=pltpu.CompilerParams(vmem_limit_bytes=32 * 2**20),
        name="pack",
    )(occ, virt_row, amplitudes)


C_STEP = 4


def ladder_prep_body(virt_s, virt_ref, table_ref, v_ref, out_ref, index_ref, perm_ref):
    step = pl.program_id(0)
    wide = NV * PART_A
    first_a = lax.axis_index("tile") * PART_A

    @pl.when(step == 0)
    def _():
        col = column_of(virt_ref[...])
        sub = iota((wide, NV), 0)
        lane = iota((wide, NV), 1)
        of_d = spread(lane == sub // PART_A, col)
        of_a = spread(lane == first_a + sub % PART_A, col)
        both = of_d ^ of_a
        table = table_ref[0:8]
        for irrep in range(IRREPS):
            index_ref[irrep] = pick_rows(table, both ^ irrep)
        repeat = iota((NV, wide), 1) // PART_A == iota((NV, wide), 0)
        irrep_row = spread(jnp.broadcast_to(virt_ref[...], (8, NV)), repeat)[0:1]
        rank_row = spread(table_ref[8:16], repeat)[0:1]
        at = iota((IRREPS * SLOTS, wide), 0)
        perm_ref[...] = jnp.where((irrep_row == at // SLOTS) & (rank_row == at % SLOTS), 1.0, 0.0).astype(BF16)

    own = iota((wide, NV), 1) // SLOTS == iota((wide, NV), 0) % PART_A
    for u in range(C_STEP):
        c = step * C_STEP + u
        irrep_c = virt_s[lax.axis_index("grp") * PART_C + c]
        got = lanes_at(v_ref[u].astype(F32), index_ref[irrep_c])
        compact = jnp.where(own, got, 0.0).astype(BF16)
        ordered = jnp.dot(perm_ref[...], compact, preferred_element_type=F32).astype(BF16)
        start = pl.multiple_of((c % 8) * NV + (c // 8) * SLOTS, SLOTS)
        for irrep in range(IRREPS):
            out_ref[irrep_c ^ irrep, pl.ds(start, SLOTS)] = ordered[irrep * SLOTS : (irrep + 1) * SLOTS]


def ladder_prep(virt, virt_row, table, ladder_rows):
    wide = NV * PART_A
    return pl.pallas_call(
        ladder_prep_body,
        grid=(PART_C // C_STEP,),
        out_shape=jax.ShapeDtypeStruct((IRREPS, PART_C * SLOTS, NV), BF16),
        in_specs=[
            pl.BlockSpec(memory_space=pltpu.SMEM),
            pl.BlockSpec((1, NV), lambda s: (0, 0)),
            pl.BlockSpec((16, NV), lambda s: (0, 0)),
            pl.BlockSpec((C_STEP, wide, NV), lambda s: (s, 0, 0)),
        ],
        out_specs=pl.BlockSpec((IRREPS, PART_C * SLOTS, NV), lambda s: (0, 0, 0)),
        scratch_shapes=[
            pltpu.VMEM((IRREPS, wide, NV), I32),
            pltpu.VMEM((IRREPS * SLOTS, wide), BF16),
        ],
        compiler_params=pltpu.CompilerParams(vmem_limit_bytes=40 * 2**20),
        cost_estimate=pl.CostEstimate(flops=2 * 10**9, bytes_accessed=7 * 10**6, transcendentals=0),
        name="ladder_prep",
    )(virt, virt_row, table, ladder_rows)


KC = NO * PART_C
KC_STEP = 64


def cycle_prep_body(w_ref, out_ref, rows_ref):
    for u in range(KC_STEP // 16):
        rows_ref[u] = w_ref[16 * u : 16 * u + 16].astype(F32).reshape(16 * NO, NV)
        for j in range(NO):
            out_ref[j, 16 * u : 16 * u + 16] = rows_ref[u, pl.ds(j, 16, stride=NO)].astype(BF16)


def cycle_prep(cycle_rows):
    return pl.pallas_call(
        cycle_prep_body,
        grid=(KC // KC_STEP,),
        out_shape=jax.ShapeDtypeStruct((NO, KC, NV), BF16),
        in_specs=[pl.BlockSpec((KC_STEP, NO, NV), lambda s: (s, 0, 0))],
        out_specs=pl.BlockSpec((NO, KC_STEP, NV), lambda s: (0, s, 0)),
        scratch_shapes=[pltpu.VMEM((KC_STEP // 16, 16 * NO, NV), F32)],
        compiler_params=pltpu.CompilerParams(vmem_limit_bytes=40 * 2**20),
        cost_estimate=pl.CostEstimate(flops=2 * 10**9, bytes_accessed=38 * 10**6, transcendentals=0),
        name="cycle_prep",
    )(cycle_rows)


J_STEP = 4
I_STEP = 6


def contract_body(occ_s, virt_ref, table_ref, t_ref, v_ref, w_ref, out_ref, ladder_ref, cut_ref, left_ref, index_ref, total_ref):
    step = pl.program_id(0)
    first_a = lax.axis_index("tile") * PART_A
    first_c = lax.axis_index("grp") * PART_C
    lane48 = iota((NO, NV), 1)

    @pl.when(step == 0)
    def _():
        sub48 = iota((NO, NV), 0)
        occ_col = jnp.zeros((NO, NV), I32)
        for i in range(NO):
            occ_col = jnp.where(sub48 == i, occ_s[i], occ_col)
        table = table_ref[0:8]
        virt8 = jnp.broadcast_to(virt_ref[...], (8, NV))
        sub = iota((NV, NV), 0)
        lane = iota((NV, NV), 1)
        of_a = sub == first_a + lane // PART_C
        of_c = sub == first_c + lane % PART_C
        a_irrep = spread(virt8, of_a)
        ac_irrep = (a_irrep ^ spread(virt8, of_c))[0:1]
        a_rank = spread(table_ref[8:16], of_a)[0:1]
        deep = (PART_C * SLOTS, NV)
        at = iota(deep, 0)
        c_at = 8 * ((at % NV) // SLOTS) + at // NV
        cut = jnp.where((c_at == iota(deep, 1) % PART_C) & (a_rank == at % SLOTS), 1.0, 0.0).astype(BF16)
        lane_g = lane48
        for a in range(PART_A):
            irrep_a = a_irrep[0:1, a * PART_C : a * PART_C + 1]
            base = occ_col ^ irrep_a
            for irrep in range(IRREPS):
                index_ref[irrep, a * NO : (a + 1) * NO] = pick_rows(table, base ^ irrep)

        def block(n, carry):
            got = t_ref[pl.ds(n * (I_STEP * 6), I_STEP * 6)].astype(F32)
            m_rows = I_STEP * NO
            planes = [
                got[:, m // 2, (m % 2) * 8 : (m % 2) * 8 + 8].reshape(m_rows, NV).astype(BF16)
                for m in range(8)
            ]
            left = jnp.concatenate(planes, axis=1)
            pair_irrep = jnp.concatenate([occ_col ^ occ_s[n * I_STEP + u] for u in range(I_STEP)], axis=0)
            total = jnp.zeros((m_rows, NV), F32)
            for pair in range(4):
                right = jnp.concatenate([v_ref[2 * pair], v_ref[2 * pair + 1]], axis=1)
                both = jnp.dot(left, right, preferred_element_type=F32)
                total = jnp.where(pair_irrep == 2 * pair, both[:, :NV], total)
                total = jnp.where(pair_irrep == 2 * pair + 1, both[:, NV:], total)
            rows = pl.ds(pl.multiple_of(n * m_rows, m_rows), m_rows)
            ladder_ref[rows] = total
            piece = jnp.dot(left, cut, preferred_element_type=F32)
            cut_ref[rows] = jnp.where(pair_irrep == ac_irrep, piece, 0.0)
            return carry

        lax.fori_loop(0, NO // I_STEP, block, 0)
        for chunk in range(NO // 4):
            parts = [cut_ref[pl.ds(4 * chunk + u, NO, stride=NO)] for u in range(4)]
            turned = [
                [parts[u] if d == 0 else pltpu.roll(parts[u], PART_C * d, 1) for d in range(4)]
                for u in range(4)
            ]
            for a in range(PART_A):
                piece = turned[3][(3 - a) % 4]
                for u in (2, 1, 0):
                    piece = jnp.where(lane48 // PART_C == u, turned[u][(u - a) % 4], piece)
                left_ref[a * NO : (a + 1) * NO, chunk * NV : (chunk + 1) * NV] = piece.astype(BF16)

    for u in range(J_STEP // 2):
        right = jnp.concatenate([w_ref[2 * u], w_ref[2 * u + 1]], axis=1)
        both = jnp.dot(left_ref[...], right, preferred_element_type=F32)
        for odd in range(2):
            j = step * J_STEP + 2 * u + odd
            got = lanes_at(both[:, odd * NV : (odd + 1) * NV], index_ref[occ_s[j]])
            value = got[3 * NO :]
            for a in (2, 1, 0):
                value = jnp.where(lane48 // SLOTS == a, got[a * NO : (a + 1) * NO], value)
            value = value + 0.5 * ladder_ref[pl.ds(j, NO, stride=NO)]
            total_ref[pl.ds(pl.multiple_of(j * NO, NO), NO)] = value

    @pl.when(step == pl.num_programs(0) - 1)
    def _():
        def anti(j, carry):
            rows = pl.ds(pl.multiple_of(j * NO, NO), NO)
            out_ref[j] = total_ref[rows] - total_ref[pl.ds(j, NO, stride=NO)]
            return carry

        lax.fori_loop(0, NO, anti, 0, unroll=4)


def contract(occ, virt_row, table, gathered, ladder_compact, cycle_compact):
    pairs = NO * NO
    return pl.pallas_call(
        contract_body,
        grid=(NO // J_STEP,),
        out_shape=jax.ShapeDtypeStruct((NO, NO, NV), F32),
        in_specs=[
            pl.BlockSpec(memory_space=pltpu.SMEM),
            pl.BlockSpec((1, NV), lambda s: (0, 0)),
            pl.BlockSpec((16, NV), lambda s: (0, 0)),
            pl.BlockSpec(gathered.shape, lambda s: (0, 0, 0, 0), pipeline_mode=pl.Buffered(1)),
            pl.BlockSpec(ladder_compact.shape, lambda s: (0, 0, 0), pipeline_mode=pl.Buffered(1)),
            pl.BlockSpec((J_STEP, KC, NV), lambda s: (s, 0, 0)),
        ],
        out_specs=pl.BlockSpec((NO, NO, NV), lambda s: (0, 0, 0)),
        scratch_shapes=[
            pltpu.VMEM((pairs, NV), F32),
            pltpu.VMEM((pairs, NV), F32),
            pltpu.VMEM((PART_A * NO, KC), BF16),
            pltpu.VMEM((IRREPS, PART_A * NO, NV), I32),
            pltpu.VMEM((pairs, NV), F32),
        ],
        compiler_params=pltpu.CompilerParams(vmem_limit_bytes=48 * 2**20),
        name="contract",
    )(occ, virt_row, table, gathered, ladder_compact, cycle_compact)


def expand_body(occ_s, virt_ref, table_ref, z_ref, out_ref):
    first_a = lax.axis_index("tile") * PART_A
    first_j = lax.axis_index("grp") * PART_J
    sub48 = iota((NO, NV), 0)
    occ_col = jnp.zeros((NO, NV), I32)
    for i in range(NO):
        occ_col = jnp.where(sub48 == i, occ_s[i], occ_col)
    virt_row = jnp.broadcast_to(virt_ref[...], (NO, NV))
    rank_row = jnp.broadcast_to(table_ref[8:9], (NO, NV))
    virt8 = jnp.broadcast_to(virt_ref[...], (8, NV))
    a_irrep = spread(virt8, iota((NV, NV), 0) == first_a + iota((NV, NV), 1) // PART_C)

    def one(j, carry):
        irrep_j = occ_s[first_j + j]
        for a in range(PART_A):
            got = lanes_at(z_ref[j], rank_row + a * SLOTS)
            want = virt_row ^ a_irrep[0:1, a * PART_C : a * PART_C + 1] ^ irrep_j
            out_ref[a, j] = jnp.where(occ_col == want, got, 0.0)
        return carry

    lax.fori_loop(0, PART_J, one, 0)


def expand(occ, virt_row, table, reduced):
    return pl.pallas_call(
        expand_body,
        out_shape=jax.ShapeDtypeStruct((PART_A, PART_J, NO, NV), F32),
        in_specs=[pl.BlockSpec(memory_space=pltpu.SMEM)] + [pl.BlockSpec(memory_space=pltpu.VMEM)] * 3,
        out_specs=pl.BlockSpec(memory_space=pltpu.VMEM),
        compiler_params=pltpu.CompilerParams(vmem_limit_bytes=32 * 2**20),
        name="expand",
    )(occ, virt_row, table, reduced)


def shards(amplitudes, ladder_ints, cycle_ints, occ_irrep, virt_irrep):
    virt_row = virt_irrep.reshape(1, NV)
    packed, table = pack(occ_irrep, virt_row, amplitudes)
    gathered = lax.all_gather(packed, "tile", axis=0, tiled=True)
    ladder_compact = ladder_prep(virt_irrep, virt_row, table, ladder_ints.reshape(PART_C, NV * PART_A, NV))
    cycle_compact = cycle_prep(cycle_ints.reshape(KC, NO, NV))
    partial_sum = contract(occ_irrep, virt_row, table, gathered, ladder_compact, cycle_compact)
    reduced = lax.psum_scatter(partial_sum, "grp", scatter_dimension=0, tiled=True)
    dense = expand(occ_irrep, virt_row, table, reduced)
    swapped = lax.all_to_all(dense, "tile", split_axis=3, concat_axis=0, tiled=True)
    return jnp.transpose(dense, (2, 1, 0, 3)) - jnp.transpose(swapped, (2, 1, 3, 0))


def solution(mesh):
    placed = (
        P("tile", "grp", None),
        P("grp", None, "tile", None),
        P(None, "grp", None, None),
        P(),
        P(),
    )
    return jax.shard_map(
        shards, mesh=mesh, in_specs=placed, out_specs=P(None, "grp", "tile", None), check_vma=False
    )
```

```python
import jax
import jax.numpy as jnp
from jax import lax
from jax.experimental import pallas as pl
from jax.experimental.pallas import tpu as pltpu
from jax.sharding import PartitionSpec as P

NO = 48
NV = 128
SLOTS = 32
PART_C = 32
PART_A = 4
PART_J = 12
TILES = 32
GRPS = 4
ROWS = 72
TURN = 24
OWN = PART_J * TURN
SHARE = OWN // TILES
PITCH = 16
MESH = pl.DeviceIdType.MESH
IRREPS = 8
F32 = jnp.float32
BF16 = jnp.bfloat16
I32 = jnp.int32


def iota(shape, axis):
    return lax.broadcasted_iota(I32, shape, axis)


def lanes_at(values, index):
    return jnp.take_along_axis(values, index, axis=1, mode="promise_in_bounds")


def spread(selector, values):
    return jnp.dot(selector.astype(BF16), values.astype(BF16), preferred_element_type=F32).astype(I32)


def pick_rows(table, which):
    picked = jnp.broadcast_to(table[0:1], which.shape)
    for irrep in range(1, IRREPS):
        picked = jnp.where(which == irrep, jnp.broadcast_to(table[irrep : irrep + 1], which.shape), picked)
    return picked


def column_of(virt_row):
    return jnp.broadcast_to(virt_row, (NV, NV)).astype(F32).T.astype(I32)


def occupied_column(occ_s, first, rows):
    sub = iota((rows, NV), 0)
    column = jnp.zeros((rows, NV), I32)
    for i in range(rows):
        at = i if isinstance(first, int) else lax.rem(first + i, NO)
        column = jnp.where(sub == i, occ_s[at], column)
    return column


def slot_tables(virt_row):
    row = jnp.broadcast_to(virt_row, (NV, NV))
    col = column_of(virt_row)
    sub = iota((NV, NV), 0)
    lane = iota((NV, NV), 1)
    same = row == col
    rank_col = jnp.sum(jnp.where(same & (lane < sub), 1.0, 0.0), axis=1, keepdims=True)
    rank_row = jnp.sum(jnp.where(same & (sub < lane), 1.0, 0.0), axis=0, keepdims=True)
    hit = jnp.broadcast_to(rank_col, (NV, NV)).astype(I32) == lane % SLOTS
    subf = sub.astype(F32)
    entries = [
        jnp.sum(jnp.where(hit & (col == irrep), subf, 0.0), axis=0, keepdims=True)
        for irrep in range(IRREPS)
    ]
    table = jnp.concatenate(entries, axis=0).astype(I32)
    return col, table, jnp.broadcast_to(rank_row, (8, NV)).astype(I32)


def pack_rows(occ_s, t_ref, index_ref, rows_ref, out_ref, me):
    first = lax.axis_index("tile") * ROWS
    quarter = iota((8, NV), 1) // SLOTS

    def one_row(r, carry):
        pair = first + r
        irrep = occ_s[pair // NO] ^ occ_s[pair % NO]
        got = lanes_at(t_ref[r].astype(F32), index_ref[irrep])
        row = got[24:32]
        for q in (2, 1, 0):
            row = jnp.where(quarter == q, got[8 * q : 8 * q + 8], row)
        rows_ref[pl.ds(pl.multiple_of(r * 8, 8), 8)] = row
        return carry

    lax.fori_loop(0, ROWS, one_row, 0, unroll=8)
    for block in range(ROWS // 8):
        for half in range(4):
            pair_of = [
                rows_ref[pl.ds(block * 64 + 2 * half + odd, 8, stride=8)] for odd in range(2)
            ]
            out_ref[me, half, block] = jnp.concatenate(pair_of, axis=0).astype(BF16)


class Ring:
    def __init__(self, t_all, send_sem, recv_sem):
        tile = lax.axis_index("tile")
        self.at = (tile // 8, (tile // 2) % 4, tile % 2)
        self.buffer, self.send_sem, self.recv_sem = t_all, send_sem, recv_sem
        self.named = {}
        self.started = []

    def tile_of(self, dx, dz, core):
        x, z, _ = self.at
        return ((x + dx + 4) % 4 * 4 + (z + dz + 4) % 4) * 2 + core

    def copy(self, name, origin, parts, target, core_of):
        number = self.named.setdefault(name, len(self.named))
        block = self.buffer.at[self.tile_of(origin[0], origin[1], core_of), parts[0] : parts[1]]
        return pltpu.make_async_remote_copy(
            src_ref=block,
            dst_ref=block,
            send_sem=self.send_sem.at[number],
            recv_sem=self.recv_sem.at[number],
            device_id={"tile": target},
            device_id_type=MESH,
        )

    def send(self, name, origin, parts, step):
        core = self.at[2]
        if step is None:
            copy = self.copy(name, origin, parts, self.tile_of(0, 0, 1 - core), core)
        else:
            copy = self.copy(name, origin, parts, self.tile_of(step[0], step[1], core), core)
        copy.start()
        self.started.append(copy)

    def arrive(self, name, origin, parts, core_of=None):
        core = self.at[2]
        self.copy(name, origin, parts, self.tile_of(0, 0, 1 - core), core if core_of is None else core_of).wait_recv()


def gather_steps(ring):
    def place(family, first, second):
        return (first, second) if family == 0 else (second, first)

    def both(family):
        return (2 * family, 2 * family + 2)

    def part(family, which):
        return (2 * family + which, 2 * family + which + 1)

    def begin():
        for family in range(2):
            ring.send((family, "f", 1), (0, 0), both(family), place(family, 1, 0))
            ring.send((family, "f", -1), (0, 0), both(family), place(family, -1, 0))
        for family in range(2):
            for step in (1, -1):
                ring.send((family, "s", 0, step), (0, 0), both(family), place(family, 0, step))
        for family in range(2):
            ring.send((family, "c", 0, 0), (0, 0), both(family), None)

    def spread_first(family, k):
        for step in (1, -1):
            ring.send((family, "s", k, step), place(family, k, 0), both(family), place(family, 0, step))
        ring.send((family, "c", k, 0), place(family, k, 0), both(family), None)

    def near():
        for family in range(2):
            for step in (1, -1):
                origin = place(family, -step, 0)
                ring.arrive((family, "f", step), origin, both(family))
                ring.send((family, "g", step), origin, part(family, 0 if step == 1 else 1), place(family, step, 0))
        for family in range(2):
            for k in (-1, 1):
                spread_first(family, k)

    def far():
        for family in range(2):
            for step in (1, -1):
                ring.arrive((family, "g", step), place(family, 2, 0), part(family, 0 if step == 1 else 1))
            spread_first(family, 2)

    def second(k):
        def run():
            for family in range(2):
                for step in (1, -1):
                    origin = place(family, k, -step)
                    ring.arrive((family, "s", k, step), origin, both(family))
                    ring.send((family, "t", k, step), origin, part(family, 0 if step == 1 else 1), place(family, 0, step))
                    ring.send((family, "c", k, -step), origin, both(family), None)

        return run

    def last(k):
        def run():
            for family in range(2):
                for step in (1, -1):
                    ring.arrive((family, "t", k, step), place(family, k, 2), part(family, 0 if step == 1 else 1))
                ring.send((family, "c", k, 2), place(family, k, 2), both(family), None)

        return run

    def siblings():
        for family in range(2):
            for k in (0, -1, 1, 2):
                for m in (0, -1, 1, 2):
                    ring.arrive((family, "c", k, m), place(family, k, m), both(family), 1 - ring.at[2])

    def settle():
        for copy in ring.started:
            copy.wait_send()

    ks = (0, -1, 1, 2)
    return [begin, near, far] + [second(k) for k in ks] + [last(k) for k in ks] + [siblings, settle]


TRANSFERS = 72
C_STEP = 4
KC = NO * PART_C
JP = NO // 2
JP_STEP = 4


def contract_body(
    occ_s, virt_s, virt_ref, t_ref, v_hbm, w_hbm, out_ref, table_ref,
    t_all, w_all, v_all, v_sem, w_sem, send_sem, recv_sem,
    index_ref, column_ref, rows_ref, v_index_ref, perm_ref, sorted_ref, right_ref,
    ladder_ref, cut_ref, left_ref, c_index_ref, total_ref,
):
    wide = NV * PART_A
    tile = lax.axis_index("tile")
    first_a = tile * PART_A
    first_c = lax.axis_index("grp") * PART_C
    v_copies = [
        pltpu.make_async_copy(v_hbm.at[pl.ds(C_STEP * n, C_STEP)], v_all.at[pl.ds(C_STEP * n, C_STEP)], v_sem.at[n])
        for n in range(PART_C // C_STEP)
    ]
    w_copies = [pltpu.make_async_copy(w_hbm.at[:, n], w_all.at[n], w_sem.at[n]) for n in range(JP)]
    for copy in v_copies + w_copies:
        copy.start()

    ring = Ring(t_all, send_sem, recv_sem)
    steps = gather_steps(ring)
    core = ring.at[2]
    barrier = pltpu.get_barrier_semaphore()
    for target in (
        ring.tile_of(1, 0, core), ring.tile_of(-1, 0, core), ring.tile_of(0, 1, core),
        ring.tile_of(0, -1, core), ring.tile_of(0, 0, 1 - core),
    ):
        pl.semaphore_signal(barrier, inc=1, device_id={"tile": target}, device_id_type=MESH)

    col, table, rank = slot_tables(virt_ref[...])
    column_ref[...] = col
    table_ref[0:8] = table
    table_ref[8:16] = rank
    c_col = column_ref[pl.ds(pl.multiple_of(first_c, PART_C), PART_C)]
    for irrep in range(IRREPS):
        index_ref[irrep] = pick_rows(table, c_col ^ irrep)
    pack_rows(occ_s, t_ref, index_ref, rows_ref, t_all, tile)
    pl.semaphore_wait(barrier, 5)
    steps[0]()

    sub = iota((wide, NV), 0)
    lane = iota((wide, NV), 1)
    of_d = spread(lane == sub // PART_A, col)
    of_a = spread(lane == first_a + sub % PART_A, col)
    both_irreps = of_d ^ of_a
    for irrep in range(IRREPS):
        v_index_ref[irrep] = pick_rows(table, both_irreps ^ irrep)
    repeat = iota((NV, wide), 1) // PART_A == iota((NV, wide), 0)
    virt8 = jnp.broadcast_to(virt_ref[...], (8, NV))
    irrep_row = spread(virt8, repeat)[0:1]
    rank_row = spread(rank, repeat)[0:1]
    at = iota((IRREPS * SLOTS, wide), 0)
    perm_ref[...] = jnp.where((irrep_row == at // SLOTS) & (rank_row == at % SLOTS), 1.0, 0.0).astype(BF16)
    steps[1]()

    def prep(c, carry):
        own = iota((wide, NV), 1) // SLOTS == iota((wide, NV), 0) % PART_A
        irrep_c = virt_s[first_c + c]
        got = lanes_at(v_all[c].astype(F32), v_index_ref[irrep_c])
        compact = jnp.where(own, got, 0.0).astype(BF16)
        ordered = jnp.dot(perm_ref[...], compact, preferred_element_type=F32).astype(BF16)
        sorted_ref[...] = ordered.reshape(IRREPS, SLOTS, NV)
        start = pl.multiple_of((c % 8) * NV + (c // 8) * SLOTS, SLOTS)
        for irrep in range(IRREPS):
            right_ref[irrep // 2, pl.ds(start, SLOTS), (irrep % 2) * NV : (irrep % 2 + 1) * NV] = sorted_ref[irrep_c ^ irrep]
        return carry

    for n in range(PART_C // C_STEP):
        v_copies[n].wait()
        lax.fori_loop(C_STEP * n, C_STEP * (n + 1), prep, 0)
        steps[2 + n]()

    occ_col = occupied_column(occ_s, 0, NO)
    subd = iota((NV, 2 * NV), 0)
    laned = iota((NV, 2 * NV), 1)
    of_a2 = subd == first_a + laned // (2 * PART_C)
    of_c2 = subd == first_c + (laned // 2) % PART_C
    a_irrep = spread(virt8, of_a2)
    ac_irrep = (a_irrep ^ spread(virt8, of_c2))[0:1]
    a_rank = spread(rank, of_a2)[0:1]
    deep = (PART_C * SLOTS, 2 * NV)
    row_at = iota(deep, 0)
    lane_at = iota(deep, 1)
    c_at = 8 * ((row_at % NV) // SLOTS) + row_at // NV
    wanted = (c_at == (lane_at // 2) % PART_C) & (lane_at % 2 == 0) & (a_rank == row_at % SLOTS)
    cut = jnp.where(wanted, 1.0, 0.0).astype(BF16)
    for a in range(PART_A):
        base = occ_col ^ a_irrep[0:1, 2 * a * PART_C : 2 * a * PART_C + 1]
        for irrep in range(IRREPS):
            c_index_ref[irrep, a * NO : (a + 1) * NO] = pick_rows(table, base ^ irrep)
    for n in range(2 + PART_C // C_STEP, len(steps) - 1):
        steps[n]()

    chips = 4
    m_rows = chips * 2 * ROWS

    def ladder_block(n, carry):
        got = t_all[pl.ds(n * 2 * chips, 2 * chips)].astype(F32)
        planes = [
            got[:, m // 2, :, (m % 2) * 8 : (m % 2) * 8 + 8].reshape(m_rows, NV).astype(BF16)
            for m in range(8)
        ]
        left = jnp.concatenate(planes, axis=1)
        pair_irrep = jnp.concatenate([occ_col ^ occ_s[n * (m_rows // NO) + u] for u in range(m_rows // NO)], axis=0)
        total = jnp.zeros((m_rows, NV), F32)
        for pair in range(4):
            both = jnp.dot(left, right_ref[pair], preferred_element_type=F32)
            total = jnp.where(pair_irrep == 2 * pair, both[:, :NV], total)
            total = jnp.where(pair_irrep == 2 * pair + 1, both[:, NV:], total)
        rows = pl.ds(pl.multiple_of(n * m_rows, m_rows), m_rows)
        ladder_ref[rows] = total
        piece = jnp.dot(left, cut, preferred_element_type=F32)
        for half in range(2):
            lanes = slice(half * NV, (half + 1) * NV)
            cut_ref[half, rows] = jnp.where(pair_irrep == ac_irrep[:, lanes], piece[:, lanes], 0.0)
        return carry

    lax.fori_loop(0, 16 // chips, ladder_block, 0)

    lane48 = iota((NO, NV), 1)
    odd_half = lane48 // (2 * PART_C) == 1

    def left_block(chunk, carry):
        for half in range(2):
            lower = cut_ref[half, pl.ds(2 * chunk, NO, stride=NO)]
            upper = cut_ref[half, pl.ds(2 * chunk + 1, NO, stride=NO)]
            even_a = jnp.where(odd_half, pltpu.roll(upper, 2 * PART_C, 1), lower)
            odd_a = jnp.where(odd_half, upper, pltpu.roll(lower, 2 * PART_C, 1))
            for odd, piece in enumerate((even_a, odd_a)):
                a = 2 * half + odd
                lanes = pl.ds(pl.multiple_of(chunk * NV, NV), NV)
                left_ref[a * NO : (a + 1) * NO, lanes] = piece.astype(BF16)
                left_ref[(PART_A + a) * NO : (PART_A + a + 1) * NO, lanes] = pltpu.roll(piece, 1, 1).astype(BF16)
        return carry

    lax.fori_loop(0, JP, left_block, 0, unroll=2)

    flat = w_all.reshape(JP * 2 * KC, NV)
    span = 2 * NO
    for copy in w_copies:
        copy.wait()

    def cycle_block(n, carry):
        right = jnp.concatenate(
            [flat[pl.ds(pl.multiple_of((n * JP_STEP + u) * 2 * KC, 2 * KC), 2 * KC)] for u in range(JP_STEP)], axis=1
        )
        both = jnp.dot(left_ref[...], right, preferred_element_type=F32)
        for u in range(JP_STEP):
            for odd in range(2):
                j = (n * JP_STEP + u) * 2 + odd
                rows = both[odd * PART_A * NO : (odd + 1) * PART_A * NO, u * NV : (u + 1) * NV]
                got = lanes_at(rows, c_index_ref[occ_s[j]])
                value = got[3 * NO :]
                for a in (2, 1, 0):
                    value = jnp.where(lane48 // SLOTS == a, got[a * NO : (a + 1) * NO], value)
                value = value + 0.5 * ladder_ref[pl.ds(j, NO, stride=NO)]
                start = pl.multiple_of(j * span, NO)
                total_ref[pl.ds(start, NO)] = value
                total_ref[pl.ds(start + NO, NO)] = value
        return carry

    lax.fori_loop(0, JP // JP_STEP, cycle_block, 0)
    total_ref[pl.ds(NO * span, TURN * span)] = total_ref[pl.ds(0, TURN * span)]

    def anti(j, carry):
        ahead = total_ref[pl.ds(j * span + j + 1, TURN, stride=1)]
        across = total_ref[pl.ds((j + 1) * span + j, TURN, stride=span)]
        out_ref[j] = ahead - across
        return carry

    lax.fori_loop(0, NO, anti, 0, unroll=4)
    steps[-1]()


def contract(occ, virt, virt_row, amplitudes, ladder_rows, cycle_pairs):
    wide = NV * PART_A
    pairs = NO * NO
    vmem = pl.BlockSpec(memory_space=pltpu.VMEM)
    smem = pl.BlockSpec(memory_space=pltpu.SMEM)
    hbm = pl.BlockSpec(memory_space=pl.ANY)
    return pl.pallas_call(
        contract_body,
        out_shape=(
            jax.ShapeDtypeStruct((NO, TURN, NV), F32),
            jax.ShapeDtypeStruct((16, NV), I32),
        ),
        in_specs=[smem, smem, vmem, vmem, hbm, hbm],
        out_specs=(vmem, vmem),
        scratch_shapes=[
            pltpu.VMEM((TILES, 4, ROWS // 8, 16, NV), BF16),
            pltpu.VMEM((JP, KC, 2, NV), BF16),
            pltpu.VMEM((PART_C, wide, NV), BF16),
            pltpu.SemaphoreType.DMA((PART_C // C_STEP,)),
            pltpu.SemaphoreType.DMA((JP,)),
            pltpu.SemaphoreType.DMA((TRANSFERS,)),
            pltpu.SemaphoreType.DMA((TRANSFERS,)),
            pltpu.VMEM((IRREPS, PART_C, NV), I32),
            pltpu.VMEM((NV, NV), I32),
            pltpu.VMEM((ROWS * 8, NV), F32),
            pltpu.VMEM((IRREPS, wide, NV), I32),
            pltpu.VMEM((IRREPS * SLOTS, wide), BF16),
            pltpu.VMEM((IRREPS, SLOTS, NV), BF16),
            pltpu.VMEM((4, PART_C * SLOTS, 2 * NV), BF16),
            pltpu.VMEM((pairs, NV), F32),
            pltpu.VMEM((2, pairs, NV), F32),
            pltpu.VMEM((2 * PART_A * NO, 2 * KC), BF16),
            pltpu.VMEM((IRREPS, PART_A * NO, NV), I32),
            pltpu.VMEM(((NO + TURN) * 2 * NO, NV), F32),
        ],
        compiler_params=pltpu.CompilerParams(
            vmem_limit_bytes=60 * 2**20, collective_id=0, has_side_effects=True
        ),
        name="contract",
    )(occ, virt, virt_row, amplitudes, ladder_rows, cycle_pairs)


def exchange_body(
    occ_s, virt_ref, table_ref, z_ref, own_ref, near_ref, far_ref,
    stage_ref, direct_ref, merged_ref, first_ref, first_in, second_ref, second_in,
    index_ref, near_out, far_out, sum_send, sum_recv, a_send, a_recv, b_send, b_recv, f_send, f_recv,
):
    tile = lax.axis_index("tile")
    grp = lax.axis_index("grp")
    up, down, over = (grp + 1) % GRPS, (grp + 3) % GRPS, (grp + 2) % GRPS
    barrier = pltpu.get_barrier_semaphore()
    for target in (up, down, over):
        pl.semaphore_signal(barrier, inc=1, device_id={"grp": target}, device_id_type=MESH)
    for d in range(1, TILES):
        pl.semaphore_signal(barrier, inc=1, device_id={"tile": (tile + d) % TILES}, device_id_type=MESH)
    pl.semaphore_wait(barrier, TILES + 2)

    half = PART_J // 2

    def block(owner, part):
        return pl.ds(owner * PART_J + part * half, half)

    def to(axis, target, src, dst, send, recv):
        return pltpu.make_async_remote_copy(
            src_ref=src, dst_ref=dst, send_sem=send, recv_sem=recv,
            device_id={axis: target}, device_id_type=MESH,
        )

    sends = [
        to("grp", up, z_ref.at[block(over, 0)], stage_ref.at[0], sum_send.at[0], sum_recv.at[0]),
        to("grp", down, z_ref.at[block(over, 1)], stage_ref.at[1], sum_send.at[1], sum_recv.at[1]),
        to("grp", up, z_ref.at[block(up, 1)], direct_ref.at[0], sum_send.at[2], sum_recv.at[2]),
        to("grp", down, z_ref.at[block(down, 0)], direct_ref.at[1], sum_send.at[3], sum_recv.at[3]),
        to("grp", up, merged_ref.at[0], direct_ref.at[2], sum_send.at[4], sum_recv.at[4]),
        to("grp", down, merged_ref.at[1], direct_ref.at[3], sum_send.at[5], sum_recv.at[5]),
    ]
    for copy in sends[:4]:
        copy.start()

    table = table_ref[0:8]
    sub = iota((NV, NV), 0)
    lane = iota((NV, NV), 1)
    turned = sub == 4 * (lane % SLOTS) + lane // SLOTS
    rank_turned = spread(table_ref[8:16], turned)[0:1]
    irrep_turned = spread(jnp.broadcast_to(virt_ref[...], (8, NV)), turned)[0:1]
    irrep_col = column_of(irrep_turned)
    table_turned = (table % 4) * SLOTS + table // 4
    for irrep in range(IRREPS):
        index_ref[irrep] = pick_rows(table_turned, irrep_col ^ irrep)

    sends[0].wait_recv()
    merged_ref[0] = stage_ref[0] + z_ref[block(up, 0)]
    sends[4].start()
    sends[1].wait_recv()
    merged_ref[1] = stage_ref[1] + z_ref[block(down, 1)]
    sends[5].start()
    sends[2].wait_recv()
    sends[3].wait_recv()
    sends[4].wait_recv()
    sends[5].wait_recv()
    lower = z_ref[block(grp, 0)] + direct_ref[1] + direct_ref[2]
    upper = z_ref[block(grp, 1)] + direct_ref[0] + direct_ref[3]
    own_ref[0 : OWN // 2] = lower.reshape(OWN // 2, NV)
    own_ref[OWN // 2 : OWN] = upper.reshape(OWN // 2, NV)
    for u in range(TILES):
        first_ref[u] = own_ref[u * SHARE : (u + 1) * SHARE]

    def swap_all(src, dst, send, recv):
        copies = []
        for d in range(1, TILES):
            target = (tile + d) % TILES
            copy = to("tile", target, src.at[target], dst.at[pl.ds(pl.multiple_of(tile * PITCH, PITCH), SHARE)], send.at[d], recv.at[d])
            copy.start()
            copies.append(copy)
        return copies

    first_in[pl.ds(pl.multiple_of(tile * PITCH, PITCH), SHARE)] = first_ref[tile]
    copies = swap_all(first_ref, first_in, a_send, a_recv)
    for copy in copies:
        copy.wait_recv()

    quarter = iota((TILES, NV), 1) // SLOTS

    def one(n, carry):
        row = tile * SHARE + n
        j = grp * PART_J + row // TURN
        i = (j + row % TURN + 1) % NO
        irrep = occ_s[i] ^ occ_s[j]
        rows = first_in[pl.ds(n, TILES, stride=PITCH)]
        full = jnp.concatenate(
            [lanes_at(rows, jnp.broadcast_to(rank_turned + a * SLOTS, (TILES, NV))) for a in range(PART_A)], axis=0
        )
        anti = full - full.T
        got = lanes_at(anti, index_ref[irrep])
        value = got[3 * TILES :]
        for a in (2, 1, 0):
            value = jnp.where(quarter == a, got[a * TILES : (a + 1) * TILES], value)
        for t in range(TILES):
            second_ref[t, pl.ds(n, 1)] = value[t : t + 1]
        return carry

    lax.fori_loop(0, SHARE, one, 0)
    second_in[pl.ds(pl.multiple_of(tile * PITCH, PITCH), SHARE)] = second_ref[tile]
    more = swap_all(second_ref, second_in, b_send, b_recv)
    for copy in more:
        copy.wait_recv()
    for u in range(TILES):
        own_ref[u * SHARE : (u + 1) * SHARE] = second_in[u * PITCH : u * PITCH + SHARE]
    for x in range(PART_J):
        near_out[x * PART_J : (x + 1) * PART_J] = own_ref[x * TURN + 11 - x : x * TURN + 23 - x]
        far_out[x * PART_J : (x + 1) * PART_J] = own_ref[x * TURN + 23 - x : x * TURN + 35 - x]
    ends = [
        to("grp", up, near_out, near_ref, f_send.at[0], f_recv.at[0]),
        to("grp", over, far_out, far_ref, f_send.at[1], f_recv.at[1]),
    ]
    for copy in ends:
        copy.start()
    for copy in sends + copies + more:
        copy.wait_send()
    for copy in ends:
        copy.wait()


def exchange(occ, virt_row, table, partial_sum):
    vmem = pl.BlockSpec(memory_space=pltpu.VMEM)
    smem = pl.BlockSpec(memory_space=pltpu.SMEM)
    block = PART_J * PART_J
    half = (PART_J // 2, TURN, NV)
    return pl.pallas_call(
        exchange_body,
        out_shape=(
            jax.ShapeDtypeStruct((OWN, NV), F32),
            jax.ShapeDtypeStruct((block, NV), F32),
            jax.ShapeDtypeStruct((block, NV), F32),
        ),
        in_specs=[smem, vmem, vmem, vmem],
        out_specs=(vmem, vmem, vmem),
        scratch_shapes=[
            pltpu.VMEM((2,) + half, F32),
            pltpu.VMEM((4,) + half, F32),
            pltpu.VMEM((2,) + half, F32),
            pltpu.VMEM((TILES, SHARE, NV), F32),
            pltpu.VMEM((TILES * PITCH, NV), F32),
            pltpu.VMEM((TILES, SHARE, NV), F32),
            pltpu.VMEM((TILES * PITCH, NV), F32),
            pltpu.VMEM((IRREPS, NV, NV), I32),
            pltpu.VMEM((block, NV), F32),
            pltpu.VMEM((block, NV), F32),
            pltpu.SemaphoreType.DMA((6,)),
            pltpu.SemaphoreType.DMA((6,)),
            pltpu.SemaphoreType.DMA((TILES,)),
            pltpu.SemaphoreType.DMA((TILES,)),
            pltpu.SemaphoreType.DMA((TILES,)),
            pltpu.SemaphoreType.DMA((TILES,)),
            pltpu.SemaphoreType.DMA((2,)),
            pltpu.SemaphoreType.DMA((2,)),
        ],
        compiler_params=pltpu.CompilerParams(
            vmem_limit_bytes=32 * 2**20, collective_id=1, has_side_effects=True
        ),
        name="exchange",
    )(occ, virt_row, table, partial_sum)


def expand_body(occ_s, virt_ref, table_ref, own_ref, near_ref, far_ref, out_ref, rows_ref):
    first_a = lax.axis_index("tile") * PART_A
    grp = lax.axis_index("grp")
    first_j = grp * PART_J
    occ_col = occupied_column(occ_s, first_j, NO)
    virt_row = jnp.broadcast_to(virt_ref[...], (NO, NV))
    rank_row = jnp.broadcast_to(table_ref[8:9], (NO, NV))
    virt8 = jnp.broadcast_to(virt_ref[...], (8, NV))
    a_irrep = spread(virt8, iota((NV, NV), 0) == first_a + iota((NV, NV), 1) // PART_C)
    n = PART_J
    for x in range(n):
        at = rows_ref.at[x]
        at[x : x + 1] = jnp.zeros((1, NV), F32)
        if x < n - 1:
            at[x + 1 : n] = own_ref[x * TURN : x * TURN + n - 1 - x]
        if x > 0:
            at[0:x] = -own_ref[pl.ds(x - 1, x, stride=TURN - 1)]
        at[n : 2 * n] = own_ref[x * TURN + 11 - x : x * TURN + 23 - x]
        at[2 * n : 2 * n + x + 1] = own_ref[x * TURN + 23 - x : x * TURN + 24]
        if x < n - 1:
            at[2 * n + x + 1 : 3 * n] = -far_ref[pl.ds((x + 1) * n + x, n - 1 - x, stride=n)]
        at[3 * n : 4 * n] = -near_ref[pl.ds(x, n, stride=n)]
    for x in range(n):
        rows = rows_ref[x]
        irrep_j = occ_s[first_j + x]
        for a in range(PART_A):
            got = lanes_at(rows, rank_row + a * SLOTS)
            want = virt_row ^ a_irrep[0:1, a * PART_C : a * PART_C + 1] ^ irrep_j
            value = jnp.where(occ_col == want, got, 0.0)
            for b in range(GRPS):
                start = lax.rem(grp + b, GRPS) * (n * n * PART_A) + x * PART_A + a
                out_ref[pl.ds(start, n, stride=n * PART_A)] = value[b * n : (b + 1) * n]


def expand(occ, virt_row, table, own, near, far):
    vmem = pl.BlockSpec(memory_space=pltpu.VMEM)
    return pl.pallas_call(
        expand_body,
        out_shape=jax.ShapeDtypeStruct((NO * PART_J * PART_A, NV), F32),
        in_specs=[pl.BlockSpec(memory_space=pltpu.SMEM)] + [vmem] * 5,
        out_specs=vmem,
        scratch_shapes=[pltpu.VMEM((PART_J, NO, NV), F32)],
        compiler_params=pltpu.CompilerParams(vmem_limit_bytes=32 * 2**20),
        name="expand",
    )(occ, virt_row, table, own, near, far)


def shards(amplitudes, ladder_ints, cycle_ints, occ_irrep, virt_irrep):
    virt_row = virt_irrep.reshape(1, NV)
    partial_sum, table = contract(
        occ_irrep, virt_irrep, virt_row, amplitudes,
        ladder_ints.reshape(PART_C, NV * PART_A, NV), cycle_ints.reshape(KC, JP, 2, NV),
    )
    own, near, far = exchange(occ_irrep, virt_row, table, partial_sum)
    return expand(occ_irrep, virt_row, table, own, near, far).reshape(NO, PART_J, PART_A, NV)


def solution(mesh):
    placed = (
        P("tile", "grp", None),
        P("grp", None, "tile", None),
        P(None, "grp", None, None),
        P(),
        P(),
    )
    return jax.shard_map(
        shards, mesh=mesh, in_specs=placed, out_specs=P(None, "grp", "tile", None), check_vma=False
    )
```

```python
import jax
import jax.numpy as jnp
from jax import lax
from jax.experimental import pallas as pl
from jax.experimental.pallas import tpu as pltpu
from jax.sharding import PartitionSpec as P

NO = 48
NV = 128
SLOTS = 32
PART_C = 32
PART_A = 4
PART_J = 12
TILES = 32
GRPS = 4
ROWS = 72
TURN = 24
OWN = PART_J * TURN
SHARE = OWN // TILES
PITCH = 16
MESH = pl.DeviceIdType.MESH
IRREPS = 8
F32 = jnp.float32
BF16 = jnp.bfloat16
I32 = jnp.int32


def iota(shape, axis):
    return lax.broadcasted_iota(I32, shape, axis)


def lanes_at(values, index):
    return jnp.take_along_axis(values, index, axis=1, mode="promise_in_bounds")


def spread(selector, values):
    return jnp.dot(selector.astype(BF16), values.astype(BF16), preferred_element_type=F32).astype(I32)


def pick_rows(table, which):
    picked = jnp.broadcast_to(table[0:1], which.shape)
    for irrep in range(1, IRREPS):
        picked = jnp.where(which == irrep, jnp.broadcast_to(table[irrep : irrep + 1], which.shape), picked)
    return picked


def column_of(virt_row):
    return jnp.broadcast_to(virt_row, (NV, NV)).astype(F32).T.astype(I32)


def occupied_column(occ_s, first, rows):
    sub = iota((rows, NV), 0)
    column = jnp.zeros((rows, NV), I32)
    for i in range(rows):
        at = i if isinstance(first, int) else lax.rem(first + i, NO)
        column = jnp.where(sub == i, occ_s[at], column)
    return column


def slot_tables(virt_row):
    row = jnp.broadcast_to(virt_row, (NV, NV))
    col = column_of(virt_row)
    sub = iota((NV, NV), 0)
    lane = iota((NV, NV), 1)
    same = row == col
    rank_col = jnp.sum(jnp.where(same & (lane < sub), 1.0, 0.0), axis=1, keepdims=True)
    rank_row = jnp.sum(jnp.where(same & (sub < lane), 1.0, 0.0), axis=0, keepdims=True)
    hit = jnp.broadcast_to(rank_col, (NV, NV)).astype(I32) == lane % SLOTS
    subf = sub.astype(F32)
    entries = [
        jnp.sum(jnp.where(hit & (col == irrep), subf, 0.0), axis=0, keepdims=True)
        for irrep in range(IRREPS)
    ]
    table = jnp.concatenate(entries, axis=0).astype(I32)
    rank_col = jnp.broadcast_to(rank_col, (NV, NV)).astype(I32)
    return col, table, jnp.broadcast_to(rank_row, (8, NV)).astype(I32), rank_col


def pack_rows(occ_s, t_ref, index_ref, rows_ref, out_ref, me):
    first = lax.axis_index("tile") * ROWS
    quarter = iota((8, NV), 1) // SLOTS

    def one_row(r, carry):
        pair = first + r
        irrep = occ_s[pair // NO] ^ occ_s[pair % NO]
        got = lanes_at(t_ref[r].astype(F32), index_ref[irrep])
        row = got[24:32]
        for q in (2, 1, 0):
            row = jnp.where(quarter == q, got[8 * q : 8 * q + 8], row)
        rows_ref[pl.ds(pl.multiple_of(r * 8, 8), 8)] = row
        return carry

    lax.fori_loop(0, ROWS, one_row, 0, unroll=8)
    for block in range(ROWS // 8):
        for half in range(4):
            pair_of = [
                rows_ref[pl.ds(block * 64 + 2 * half + odd, 8, stride=8)] for odd in range(2)
            ]
            out_ref[me, half, block] = jnp.concatenate(pair_of, axis=0).astype(BF16)


class Ring:
    def __init__(self, t_all, send_sem, recv_sem):
        tile = lax.axis_index("tile")
        self.at = (tile // 8, (tile // 2) % 4, tile % 2)
        self.buffer, self.send_sem, self.recv_sem = t_all, send_sem, recv_sem
        self.named = {}
        self.started = []

    def tile_of(self, dx, dz, core):
        x, z, _ = self.at
        return ((x + dx + 4) % 4 * 4 + (z + dz + 4) % 4) * 2 + core

    def copy(self, name, origin, parts, target, core_of):
        number = self.named.setdefault(name, len(self.named))
        block = self.buffer.at[self.tile_of(origin[0], origin[1], core_of), parts[0] : parts[1]]
        return pltpu.make_async_remote_copy(
            src_ref=block,
            dst_ref=block,
            send_sem=self.send_sem.at[number],
            recv_sem=self.recv_sem.at[number],
            device_id={"tile": target},
            device_id_type=MESH,
        )

    def send(self, name, origin, parts, step):
        core = self.at[2]
        if step is None:
            copy = self.copy(name, origin, parts, self.tile_of(0, 0, 1 - core), core)
        else:
            copy = self.copy(name, origin, parts, self.tile_of(step[0], step[1], core), core)
        copy.start()
        self.started.append(copy)

    def arrive(self, name, origin, parts, core_of=None):
        core = self.at[2]
        self.copy(name, origin, parts, self.tile_of(0, 0, 1 - core), core if core_of is None else core_of).wait_recv()


def gather_steps(ring):
    def place(family, first, second):
        return (first, second) if family == 0 else (second, first)

    def both(family):
        return (2 * family, 2 * family + 2)

    def part(family, which):
        return (2 * family + which, 2 * family + which + 1)

    def begin():
        for family in range(2):
            ring.send((family, "f", 1), (0, 0), both(family), place(family, 1, 0))
            ring.send((family, "f", -1), (0, 0), both(family), place(family, -1, 0))
        for family in range(2):
            for step in (1, -1):
                ring.send((family, "s", 0, step), (0, 0), both(family), place(family, 0, step))
        for family in range(2):
            ring.send((family, "c", 0, 0), (0, 0), both(family), None)

    def spread_first(family, k):
        for step in (1, -1):
            ring.send((family, "s", k, step), place(family, k, 0), both(family), place(family, 0, step))
        ring.send((family, "c", k, 0), place(family, k, 0), both(family), None)

    def near():
        for family in range(2):
            for step in (1, -1):
                origin = place(family, -step, 0)
                ring.arrive((family, "f", step), origin, both(family))
                ring.send((family, "g", step), origin, part(family, 0 if step == 1 else 1), place(family, step, 0))
        for family in range(2):
            for k in (-1, 1):
                spread_first(family, k)

    def far():
        for family in range(2):
            for step in (1, -1):
                ring.arrive((family, "g", step), place(family, 2, 0), part(family, 0 if step == 1 else 1))
            spread_first(family, 2)

    def second(k):
        def run():
            for family in range(2):
                for step in (1, -1):
                    origin = place(family, k, -step)
                    ring.arrive((family, "s", k, step), origin, both(family))
                    ring.send((family, "t", k, step), origin, part(family, 0 if step == 1 else 1), place(family, 0, step))
                    ring.send((family, "c", k, -step), origin, both(family), None)

        return run

    def last(k):
        def run():
            for family in range(2):
                for step in (1, -1):
                    ring.arrive((family, "t", k, step), place(family, k, 2), part(family, 0 if step == 1 else 1))
                ring.send((family, "c", k, 2), place(family, k, 2), both(family), None)

        return run

    def sibling(origin):
        for family in range(2):
            k, m = place(family, origin[0], origin[1])
            ring.arrive((family, "c", k, m), origin, both(family), 1 - ring.at[2])

    def settle():
        for copy in ring.started:
            copy.wait_send()

    steps = {"begin": begin, "near": near, "far": far, "sibling": sibling, "settle": settle}
    for k in (0, -1, 1, 2):
        steps["second", k] = second(k)
        steps["last", k] = last(k)
    return steps


TRANSFERS = 72
KC = NO * PART_C
JP = NO // 2
JP_STEP = 4
FAR = 72


def contract_body(
    occ_s, virt_s, virt_ref, t_ref, v_hbm, w_hbm, own_ref, near_ref, far_ref, table_ref,
    t_all, w_all, v_all, v_sem, w_sem, send_sem, recv_sem,
    index_ref, column_ref, rows_ref, perm_ref, x_all, slot_ref, right_ref, cut_one_ref,
    ladder_ref, cut_ref, left_ref, c_index_ref, total_ref, both_a, both_b, z_ref, *exchange_refs,
):
    tile = lax.axis_index("tile")
    grp = lax.axis_index("grp")
    first_a = tile * PART_A
    first_c = grp * PART_C
    v_copies = [pltpu.make_async_copy(v_hbm.at[:, :, n], v_all.at[n], v_sem.at[n]) for n in range(2)]
    w_copies = [pltpu.make_async_copy(w_hbm.at[:, n], w_all.at[n], w_sem.at[n]) for n in range(JP)]
    for copy in v_copies + w_copies:
        copy.start()

    ring = Ring(t_all, send_sem, recv_sem)
    steps = gather_steps(ring)
    core = ring.at[2]
    barrier = pltpu.get_barrier_semaphore()
    for target in (
        ring.tile_of(1, 0, core), ring.tile_of(-1, 0, core), ring.tile_of(0, 1, core),
        ring.tile_of(0, -1, core), ring.tile_of(0, 0, 1 - core),
    ):
        pl.semaphore_signal(barrier, inc=1, device_id={"tile": target}, device_id_type=MESH)
    for d in range(1, GRPS):
        pl.semaphore_signal(barrier, inc=1, device_id={"grp": (grp + d) % GRPS}, device_id_type=MESH)

    col, table, rank, rank_col = slot_tables(virt_ref[...])
    column_ref[...] = col
    table_ref[0:8] = table
    table_ref[8:16] = rank
    c_col = column_ref[pl.ds(pl.multiple_of(first_c, PART_C), PART_C)]
    for irrep in range(IRREPS):
        index_ref[irrep] = pick_rows(table, c_col ^ irrep)
    pack_rows(occ_s, t_ref, index_ref, rows_ref, t_all, tile)
    pl.semaphore_wait(barrier, 8)
    steps["begin"]()

    virt8 = jnp.broadcast_to(virt_ref[...], (8, NV))
    repeat = iota((NV, 2 * NV), 1) // 2 == iota((NV, 2 * NV), 0)
    irrep_row = spread(virt8, repeat)[0:1]
    rank_row = spread(rank, repeat)[0:1]
    at = iota((2 * IRREPS * SLOTS, 2 * NV), 0)
    par = iota((2 * IRREPS * SLOTS, 2 * NV), 1) % 2
    wanted = (irrep_row == (at // SLOTS) % IRREPS) & (rank_row == at % SLOTS) & (par == at // (IRREPS * SLOTS))
    perm_ref[...] = jnp.where(wanted, 1.0, 0.0).astype(BF16)

    flat_v = v_all.reshape(2 * PART_C * 2 * NV, NV)

    def sort_rows(c, carry):
        right = jnp.concatenate(
            [flat_v[pl.ds(pl.multiple_of((p * PART_C + c) * 2 * NV, 2 * NV), 2 * NV)] for p in range(2)], axis=1
        )
        ordered = jnp.dot(perm_ref[...], right, preferred_element_type=F32).astype(BF16)
        x_all[c] = ordered.reshape(2, IRREPS, SLOTS, 2 * NV)
        return carry

    for copy in v_copies:
        copy.wait()
    lax.fori_loop(0, PART_C // 2, sort_rows, 0, unroll=4)
    steps["near"]()
    lax.fori_loop(PART_C // 2, PART_C, sort_rows, 0, unroll=4)
    steps["far"]()

    lane = iota((NV, NV), 1)
    of_a = iota((NV, NV), 0) == first_a + lane // SLOTS
    a_row = spread(virt8, of_a)[0:1]
    mixed = jnp.where(rank_col == lane % SLOTS, col ^ a_row, -1)
    for p in range(4):
        a = 2 * (p % 2) + p // 2
        mine = jnp.where(lane // SLOTS == a, mixed, -1)
        for irrep in range(IRREPS):
            slot_ref[irrep, p * NV : (p + 1) * NV] = jnp.where(mine == irrep, 1.0, 0.0).astype(BF16)

    def pick_slots(pair, carry):
        for odd in range(2):
            irrep = 2 * pair + odd
            for q in range(4):
                blocks = []
                for m in range(8):
                    c = 8 * q + m
                    which = virt_s[first_c + c] ^ irrep
                    blocks.append(jnp.concatenate([x_all[c, 0, which], x_all[c, 1, which]], axis=1))
                got = jnp.dot(jnp.concatenate(blocks, axis=0), slot_ref[irrep], preferred_element_type=F32).astype(BF16)
                for m in range(8):
                    start = m * NV + q * SLOTS
                    right_ref[pair, start : start + SLOTS, odd * NV : (odd + 1) * NV] = got[m * SLOTS : (m + 1) * SLOTS]
        return carry

    lax.fori_loop(0, 2, pick_slots, 0)
    steps["second", 0]()
    lax.fori_loop(2, 4, pick_slots, 0)
    steps["second", -1]()

    occ_col = occupied_column(occ_s, 0, NO)
    subd = iota((NV, 2 * NV), 0)
    laned = iota((NV, 2 * NV), 1)
    of_a2 = subd == first_a + laned // (2 * PART_C)
    of_c2 = subd == first_c + (laned // 2) % PART_C
    a_irrep = spread(virt8, of_a2)
    ac_irrep = (a_irrep ^ spread(virt8, of_c2))[0:1]
    a_rank = spread(rank, of_a2)[0:1]
    deep = (PART_C * SLOTS, 2 * NV)
    row_at = iota(deep, 0)
    lane_at = iota(deep, 1)
    c_at = 8 * ((row_at % NV) // SLOTS) + row_at // NV
    wanted = (c_at == (lane_at // 2) % PART_C) & (lane_at % 2 == 0) & (a_rank == row_at % SLOTS)
    cut_one_ref[...] = jnp.where(wanted, 1.0, 0.0).astype(BF16)
    for a in range(PART_A):
        base = occ_col ^ a_irrep[0:1, 2 * a * PART_C : 2 * a * PART_C + 1]
        for irrep in range(IRREPS):
            c_index_ref[irrep, a * NO : (a + 1) * NO] = pick_rows(table, base ^ irrep)

    each = 2 * ROWS

    def ladder_pair(*origins):
        for origin in origins:
            steps["sibling"](origin)
        chips = [ring.tile_of(dx, dz, 0) // 2 for dx, dz in origins]
        slabs = [t_all[pl.ds(2 * chip, 2)].astype(F32) for chip in chips]
        planes = [
            jnp.concatenate(
                [got[:, m // 2, :, (m % 2) * 8 : (m % 2) * 8 + 8].reshape(each, NV) for got in slabs], axis=0
            ).astype(BF16)
            for m in range(8)
        ]
        left = jnp.concatenate(planes, axis=1)
        pair_irrep = jnp.concatenate([occ_col ^ occ_s[3 * chip + u] for chip in chips for u in range(3)], axis=0)
        total = jnp.zeros((2 * each, NV), F32)
        for pair in range(4):
            both = jnp.dot(left, right_ref[pair], preferred_element_type=F32)
            total = jnp.where(pair_irrep == 2 * pair, both[:, :NV], total)
            total = jnp.where(pair_irrep == 2 * pair + 1, both[:, NV:], total)
        piece = jnp.dot(left, cut_one_ref[...], preferred_element_type=F32)
        for n, chip in enumerate(chips):
            rows = pl.ds(pl.multiple_of(chip * each, each), each)
            part = slice(n * each, (n + 1) * each)
            ladder_ref[rows] = total[part]
            for half in range(2):
                lanes = slice(half * NV, (half + 1) * NV)
                cut_ref[half, rows] = jnp.where(pair_irrep[part] == ac_irrep[:, lanes], piece[part, lanes], 0.0)

    ladder_pair((0, 0), (1, 0))
    steps["second", 1]()
    ladder_pair((-1, 0), (0, 1))
    steps["second", 2]()
    ladder_pair((0, -1), (-1, -1))
    steps["last", 0]()
    ladder_pair((1, 1), (-1, 1))
    steps["last", -1]()
    steps["last", 1]()
    ladder_pair((1, -1), (0, 2))
    steps["last", 2]()
    ladder_pair((2, 0), (1, 2))
    ladder_pair((-1, 2), (2, 1))
    ladder_pair((2, -1), (2, 2))

    lane48 = iota((NO, NV), 1)
    odd_half = lane48 // (2 * PART_C) == 1

    def left_block(chunk, carry):
        for half in range(2):
            lower = cut_ref[half, pl.ds(2 * chunk, NO, stride=NO)]
            upper = cut_ref[half, pl.ds(2 * chunk + 1, NO, stride=NO)]
            even_a = jnp.where(odd_half, pltpu.roll(upper, 2 * PART_C, 1), lower)
            odd_a = jnp.where(odd_half, upper, pltpu.roll(lower, 2 * PART_C, 1))
            for odd, piece in enumerate((even_a, odd_a)):
                a = 2 * half + odd
                lanes = pl.ds(pl.multiple_of(chunk * NV, NV), NV)
                left_ref[a * NO : (a + 1) * NO, lanes] = piece.astype(BF16)
                left_ref[(PART_A + a) * NO : (PART_A + a + 1) * NO, lanes] = pltpu.roll(piece, 1, 1).astype(BF16)
        return carry

    lax.fori_loop(0, JP, left_block, 0, unroll=4)

    flat = w_all.reshape(JP * 2 * KC, NV)
    span = 2 * NO
    for copy in w_copies:
        copy.wait()

    def cycle_product(n, out):
        right = jnp.concatenate(
            [flat[pl.ds(pl.multiple_of((n * JP_STEP + u) * 2 * KC, 2 * KC), 2 * KC)] for u in range(JP_STEP)], axis=1
        )
        out[...] = jnp.dot(left_ref[...], right, preferred_element_type=F32)

    def cycle_place(n, both):
        for u in range(JP_STEP):
            for odd in range(2):
                j = (n * JP_STEP + u) * 2 + odd
                rows = both[odd * PART_A * NO : (odd + 1) * PART_A * NO, u * NV : (u + 1) * NV]
                got = lanes_at(rows, c_index_ref[occ_s[j]])
                value = got[3 * NO :]
                for a in (2, 1, 0):
                    value = jnp.where(lane48 // SLOTS == a, got[a * NO : (a + 1) * NO], value)
                value = value + 0.5 * ladder_ref[pl.ds(j, NO, stride=NO)]
                start = pl.multiple_of(j * span, NO)
                total_ref[pl.ds(start, NO)] = value
                total_ref[pl.ds(start + NO, NO)] = value

    cycle_product(0, both_a)

    def cycle_pair(n, carry):
        cycle_product(2 * n + 1, both_b)
        cycle_place(2 * n, both_a)
        cycle_product(2 * n + 2, both_a)
        cycle_place(2 * n + 1, both_b)
        return carry

    blocks = JP // JP_STEP
    lax.fori_loop(0, blocks // 2 - 1, cycle_pair, 0)
    cycle_product(blocks - 1, both_b)
    cycle_place(blocks - 2, both_a)
    cycle_place(blocks - 1, both_b)
    total_ref[pl.ds(NO * span, TURN * span)] = total_ref[pl.ds(0, TURN * span)]

    def anti(j, carry):
        ahead = total_ref[pl.ds(j * span + j + 1, TURN, stride=1)]
        across = total_ref[pl.ds((j + 1) * span + j, TURN, stride=span)]
        z_ref[j] = ahead - across
        return carry

    lax.fori_loop(0, NO, anti, 0, unroll=4)
    exchange_part(occ_s, virt8, table, rank, z_ref, own_ref, near_ref, far_ref, *exchange_refs)
    steps["settle"]()


def contract(occ, virt, virt_row, amplitudes, ladder_pairs, cycle_pairs):
    pairs = NO * NO
    block = PART_J * PART_J
    half = (PART_J // 2, TURN, NV)
    vmem = pl.BlockSpec(memory_space=pltpu.VMEM)
    smem = pl.BlockSpec(memory_space=pltpu.SMEM)
    hbm = pl.BlockSpec(memory_space=pl.ANY)
    return pl.pallas_call(
        contract_body,
        out_shape=(
            jax.ShapeDtypeStruct((OWN, NV), F32),
            jax.ShapeDtypeStruct((block, NV), F32),
            jax.ShapeDtypeStruct((FAR, NV), F32),
            jax.ShapeDtypeStruct((16, NV), I32),
        ),
        in_specs=[smem, smem, vmem, vmem, hbm, hbm],
        out_specs=(vmem, vmem, vmem, vmem),
        scratch_shapes=[
            pltpu.VMEM((TILES, 4, ROWS // 8, 16, NV), BF16),
            pltpu.VMEM((JP, KC, 2, NV), BF16),
            pltpu.VMEM((2, PART_C, NV, 2, NV), BF16),
            pltpu.SemaphoreType.DMA((2,)),
            pltpu.SemaphoreType.DMA((JP,)),
            pltpu.SemaphoreType.DMA((TRANSFERS,)),
            pltpu.SemaphoreType.DMA((TRANSFERS,)),
            pltpu.VMEM((IRREPS, PART_C, NV), I32),
            pltpu.VMEM((NV, NV), I32),
            pltpu.VMEM((ROWS * 8, NV), F32),
            pltpu.VMEM((2 * IRREPS * SLOTS, 2 * NV), BF16),
            pltpu.VMEM((PART_C, 2, IRREPS, SLOTS, 2 * NV), BF16),
            pltpu.VMEM((IRREPS, 4 * NV, NV), BF16),
            pltpu.VMEM((4, PART_C * SLOTS, 2 * NV), BF16),
            pltpu.VMEM((PART_C * SLOTS, 2 * NV), BF16),
            pltpu.VMEM((pairs, NV), F32),
            pltpu.VMEM((2, pairs, NV), F32),
            pltpu.VMEM((2 * PART_A * NO, 2 * KC), BF16),
            pltpu.VMEM((IRREPS, PART_A * NO, NV), I32),
            pltpu.VMEM(((NO + TURN) * 2 * NO, NV), F32),
            pltpu.VMEM((2 * PART_A * NO, JP_STEP * NV), F32),
            pltpu.VMEM((2 * PART_A * NO, JP_STEP * NV), F32),
            pltpu.VMEM((NO, TURN, NV), F32),
            pltpu.VMEM((2,) + half, F32),
            pltpu.VMEM((4,) + half, F32),
            pltpu.VMEM((2,) + half, F32),
            pltpu.VMEM((TILES, SHARE, NV), F32),
            pltpu.VMEM((TILES * PITCH, NV), F32),
            pltpu.VMEM((TILES, SHARE, NV), F32),
            pltpu.VMEM((TILES * PITCH, NV), F32),
            pltpu.VMEM((IRREPS, NV, NV), I32),
            pltpu.VMEM((block, NV), F32),
            pltpu.VMEM((FAR, NV), F32),
            pltpu.SemaphoreType.DMA((6,)),
            pltpu.SemaphoreType.DMA((6,)),
            pltpu.SemaphoreType.DMA((TILES,)),
            pltpu.SemaphoreType.DMA((TILES,)),
            pltpu.SemaphoreType.DMA((TILES,)),
            pltpu.SemaphoreType.DMA((TILES,)),
            pltpu.SemaphoreType.DMA((2,)),
            pltpu.SemaphoreType.DMA((2,)),
        ],
        compiler_params=pltpu.CompilerParams(
            vmem_limit_bytes=62 * 2**20, collective_id=0, has_side_effects=True
        ),
        name="contract",
    )(occ, virt, virt_row, amplitudes, ladder_pairs, cycle_pairs)


def exchange_part(
    occ_s, virt8, table, rank, z_ref, own_ref, near_ref, far_ref,
    stage_ref, direct_ref, merged_ref, first_ref, first_in, second_ref, second_in,
    index_ref, near_out, far_out, sum_send, sum_recv, a_send, a_recv, b_send, b_recv, f_send, f_recv,
):
    tile = lax.axis_index("tile")
    grp = lax.axis_index("grp")
    up, down, over = (grp + 1) % GRPS, (grp + 3) % GRPS, (grp + 2) % GRPS
    half = PART_J // 2

    def block(owner, part):
        return pl.ds(owner * PART_J + part * half, half)

    def to(axis, target, src, dst, send, recv):
        return pltpu.make_async_remote_copy(
            src_ref=src, dst_ref=dst, send_sem=send, recv_sem=recv,
            device_id={axis: target}, device_id_type=MESH,
        )

    sends = [
        to("grp", up, z_ref.at[block(over, 0)], stage_ref.at[0], sum_send.at[0], sum_recv.at[0]),
        to("grp", down, z_ref.at[block(over, 1)], stage_ref.at[1], sum_send.at[1], sum_recv.at[1]),
        to("grp", up, z_ref.at[block(up, 1)], direct_ref.at[0], sum_send.at[2], sum_recv.at[2]),
        to("grp", down, z_ref.at[block(down, 0)], direct_ref.at[1], sum_send.at[3], sum_recv.at[3]),
        to("grp", up, merged_ref.at[0], direct_ref.at[2], sum_send.at[4], sum_recv.at[4]),
        to("grp", down, merged_ref.at[1], direct_ref.at[3], sum_send.at[5], sum_recv.at[5]),
    ]
    for copy in sends[:4]:
        copy.start()

    sub = iota((NV, NV), 0)
    lane = iota((NV, NV), 1)
    turned = sub == 4 * (lane % SLOTS) + lane // SLOTS
    rank_turned = spread(rank, turned)[0:1]
    irrep_turned = spread(virt8, turned)[0:1]
    irrep_col = column_of(irrep_turned)
    table_turned = (table % 4) * SLOTS + table // 4
    for irrep in range(IRREPS):
        index_ref[irrep] = pick_rows(table_turned, irrep_col ^ irrep)

    sends[0].wait_recv()
    merged_ref[0] = stage_ref[0] + z_ref[block(up, 0)]
    sends[4].start()
    sends[1].wait_recv()
    merged_ref[1] = stage_ref[1] + z_ref[block(down, 1)]
    sends[5].start()
    sends[2].wait_recv()
    sends[3].wait_recv()
    sends[4].wait_recv()
    sends[5].wait_recv()
    lower = z_ref[block(grp, 0)] + direct_ref[1] + direct_ref[2]
    upper = z_ref[block(grp, 1)] + direct_ref[0] + direct_ref[3]
    own_ref[0 : OWN // 2] = lower.reshape(OWN // 2, NV)
    own_ref[OWN // 2 : OWN] = upper.reshape(OWN // 2, NV)
    for u in range(TILES):
        first_ref[u] = own_ref[u * SHARE : (u + 1) * SHARE]

    def swap_all(src, dst, send, recv):
        copies = []
        for d in range(1, TILES):
            target = (tile + d) % TILES
            copy = to("tile", target, src.at[target], dst.at[pl.ds(pl.multiple_of(tile * PITCH, PITCH), SHARE)], send.at[d], recv.at[d])
            copy.start()
            copies.append(copy)
        return copies

    first_in[pl.ds(pl.multiple_of(tile * PITCH, PITCH), SHARE)] = first_ref[tile]
    copies = swap_all(first_ref, first_in, a_send, a_recv)
    for copy in copies:
        copy.wait_recv()

    quarter = iota((TILES, NV), 1) // SLOTS

    def one(n, carry):
        row = tile * SHARE + n
        j = grp * PART_J + row // TURN
        i = (j + row % TURN + 1) % NO
        irrep = occ_s[i] ^ occ_s[j]
        rows = first_in[pl.ds(n, TILES, stride=PITCH)]
        full = jnp.concatenate(
            [lanes_at(rows, jnp.broadcast_to(rank_turned + a * SLOTS, (TILES, NV))) for a in range(PART_A)], axis=0
        )
        anti = full - full.T
        got = lanes_at(anti, index_ref[irrep])
        value = got[3 * TILES :]
        for a in (2, 1, 0):
            value = jnp.where(quarter == a, got[a * TILES : (a + 1) * TILES], value)
        for t in range(TILES):
            second_ref[t, pl.ds(n, 1)] = value[t : t + 1]
        return carry

    lax.fori_loop(0, SHARE, one, 0, unroll=3)
    second_in[pl.ds(pl.multiple_of(tile * PITCH, PITCH), SHARE)] = second_ref[tile]
    more = swap_all(second_ref, second_in, b_send, b_recv)
    for copy in more:
        copy.wait_recv()
    for u in range(TILES):
        own_ref[u * SHARE : (u + 1) * SHARE] = second_in[u * PITCH : u * PITCH + SHARE]
    for x in range(PART_J):
        near_out[x * PART_J : (x + 1) * PART_J] = own_ref[x * TURN + 11 - x : x * TURN + 23 - x]
    far_out[FAR - 8 : FAR] = jnp.zeros((8, NV), F32)
    filled = 0
    for y in range(PART_J - 1):
        count = PART_J - 1 - y
        far_out[filled : filled + count] = own_ref[pl.ds((y + 1) * (TURN - 1) + 23 + y, count, stride=TURN - 1)]
        filled += count
    ends = [
        to("grp", up, near_out, near_ref, f_send.at[0], f_recv.at[0]),
        to("grp", over, far_out, far_ref, f_send.at[1], f_recv.at[1]),
    ]
    for copy in ends:
        copy.start()
    for copy in sends + copies + more:
        copy.wait_send()
    for copy in ends:
        copy.wait()


def expand_body(occ_s, virt_ref, table_ref, own_ref, near_ref, far_ref, out_ref, rows_ref):
    first_a = lax.axis_index("tile") * PART_A
    grp = lax.axis_index("grp")
    first_j = grp * PART_J
    occ_col = occupied_column(occ_s, first_j, NO)
    virt_row = jnp.broadcast_to(virt_ref[...], (NO, NV))
    rank_row = jnp.broadcast_to(table_ref[8:9], (NO, NV))
    virt8 = jnp.broadcast_to(virt_ref[...], (8, NV))
    a_irrep = spread(virt8, iota((NV, NV), 0) == first_a + iota((NV, NV), 1) // PART_C)
    n = PART_J
    for x in range(n):
        at = rows_ref.at[x]
        at[x : x + 1] = jnp.zeros((1, NV), F32)
        if x < n - 1:
            at[x + 1 : n] = own_ref[x * TURN : x * TURN + n - 1 - x]
        if x > 0:
            at[0:x] = -own_ref[pl.ds(x - 1, x, stride=TURN - 1)]
        at[n : 2 * n] = own_ref[x * TURN + 11 - x : x * TURN + 23 - x]
        at[2 * n : 2 * n + x + 1] = own_ref[x * TURN + 23 - x : x * TURN + 24]
        if x < n - 1:
            filled = x * (n - 1) - x * (x - 1) // 2
            at[2 * n + x + 1 : 3 * n] = -far_ref[filled : filled + n - 1 - x]
        at[3 * n : 4 * n] = -near_ref[pl.ds(x, n, stride=n)]
    for x in range(n):
        rows = rows_ref[x]
        irrep_j = occ_s[first_j + x]
        for a in range(PART_A):
            got = lanes_at(rows, rank_row + a * SLOTS)
            want = virt_row ^ a_irrep[0:1, a * PART_C : a * PART_C + 1] ^ irrep_j
            value = jnp.where(occ_col == want, got, 0.0)
            for b in range(GRPS):
                start = lax.rem(grp + b, GRPS) * (n * n * PART_A) + x * PART_A + a
                out_ref[pl.ds(start, n, stride=n * PART_A)] = value[b * n : (b + 1) * n]


def expand(occ, virt_row, table, own, near, far):
    vmem = pl.BlockSpec(memory_space=pltpu.VMEM)
    return pl.pallas_call(
        expand_body,
        out_shape=jax.ShapeDtypeStruct((NO * PART_J * PART_A, NV), F32),
        in_specs=[pl.BlockSpec(memory_space=pltpu.SMEM)] + [vmem] * 5,
        out_specs=vmem,
        scratch_shapes=[pltpu.VMEM((PART_J, NO, NV), F32)],
        compiler_params=pltpu.CompilerParams(vmem_limit_bytes=32 * 2**20),
        name="expand",
    )(occ, virt_row, table, own, near, far)


def shards(amplitudes, ladder_ints, cycle_ints, occ_irrep, virt_irrep):
    virt_row = virt_irrep.reshape(1, NV)
    own, near, far, table = contract(
        occ_irrep, virt_irrep, virt_row, amplitudes,
        ladder_ints.reshape(PART_C, NV, 2, 2, NV), cycle_ints.reshape(KC, JP, 2, NV),
    )
    return expand(occ_irrep, virt_row, table, own, near, far).reshape(NO, PART_J, PART_A, NV)


def solution(mesh):
    placed = (
        P("tile", "grp", None),
        P("grp", None, "tile", None),
        P(None, "grp", None, None),
        P(),
        P(),
    )
    return jax.shard_map(
        shards, mesh=mesh, in_specs=placed, out_specs=P(None, "grp", "tile", None), check_vma=False
    )
```

```python
import functools

import jax
import jax.numpy as jnp
from jax import lax
from jax.experimental import pallas as pl
from jax.experimental.pallas import tpu as pltpu
from jax.sharding import PartitionSpec as P

NO = 48
NV = 128
SLOTS = 32
PART_C = 32
PART_A = 4
PART_J = 12
TILES = 32
GRPS = 4
ROWS = 72
TURN = 24
OWN = PART_J * TURN
SHARE = OWN // TILES
PITCH = 16
MESH = pl.DeviceIdType.MESH
IRREPS = 8
F32 = jnp.float32
BF16 = jnp.bfloat16
I32 = jnp.int32


def iota(shape, axis):
    return lax.broadcasted_iota(I32, shape, axis)


def lanes_at(values, index):
    return jnp.take_along_axis(values, index, axis=1, mode="promise_in_bounds")


def spread(selector, values):
    return jnp.dot(selector.astype(BF16), values.astype(BF16), preferred_element_type=F32).astype(I32)


def pick_rows(table, which):
    picked = jnp.broadcast_to(table[0:1], which.shape)
    for irrep in range(1, IRREPS):
        picked = jnp.where(which == irrep, jnp.broadcast_to(table[irrep : irrep + 1], which.shape), picked)
    return picked


def column_of(virt_row):
    return jnp.broadcast_to(virt_row, (NV, NV)).astype(F32).T.astype(I32)


def occupied_column(occ_s, first, rows):
    sub = iota((rows, NV), 0)
    column = jnp.zeros((rows, NV), I32)
    for i in range(rows):
        at = i if isinstance(first, int) else lax.rem(first + i, NO)
        column = jnp.where(sub == i, occ_s[at], column)
    return column


def slot_tables(virt_row):
    row = jnp.broadcast_to(virt_row, (NV, NV))
    col = column_of(virt_row)
    sub = iota((NV, NV), 0)
    lane = iota((NV, NV), 1)
    same = row == col
    rank_col = jnp.sum(jnp.where(same & (lane < sub), 1.0, 0.0), axis=1, keepdims=True)
    rank_row = jnp.sum(jnp.where(same & (sub < lane), 1.0, 0.0), axis=0, keepdims=True)
    hit = jnp.broadcast_to(rank_col, (NV, NV)).astype(I32) == lane % SLOTS
    subf = sub.astype(F32)
    entries = [
        jnp.sum(jnp.where(hit & (col == irrep), subf, 0.0), axis=0, keepdims=True)
        for irrep in range(IRREPS)
    ]
    table = jnp.concatenate(entries, axis=0).astype(I32)
    rank_col = jnp.broadcast_to(rank_col, (NV, NV)).astype(I32)
    return col, table, jnp.broadcast_to(rank_row, (8, NV)).astype(I32), rank_col


def pack_rows(occ_s, t_ref, index_ref, rows_ref, out_ref, me):
    first = lax.axis_index("tile") * ROWS
    quarter = iota((8, NV), 1) // SLOTS

    def one_row(r, carry):
        pair = first + r
        irrep = occ_s[pair // NO] ^ occ_s[pair % NO]
        got = lanes_at(t_ref[r].astype(F32), index_ref[irrep])
        row = got[24:32]
        for q in (2, 1, 0):
            row = jnp.where(quarter == q, got[8 * q : 8 * q + 8], row)
        rows_ref[pl.ds(pl.multiple_of(r * 8, 8), 8)] = row
        return carry

    lax.fori_loop(0, ROWS, one_row, 0, unroll=8)
    for block in range(ROWS // 8):
        for half in range(4):
            pair_of = [
                rows_ref[pl.ds(block * 64 + 2 * half + odd, 8, stride=8)] for odd in range(2)
            ]
            out_ref[me, half, block] = jnp.concatenate(pair_of, axis=0).astype(BF16)


PAIRED = (
    ((0, 0), (1, 0)), ((-1, 0), (0, 1)), ((0, -1), (-1, -1)), ((1, 1), (-1, 1)),
    ((1, -1), (0, 2)), ((2, 0), (1, 2)), ((-1, 2), (2, 1)), ((2, -1), (2, 2)),
)
RING_COPIES = 40


class Ring:
    def __init__(self, t_all, send_sem, recv_sem):
        tile = lax.axis_index("tile")
        self.at = (tile // 8, (tile // 2) % 4, tile % 2)
        self.buffer, self.send_sem, self.recv_sem = t_all, send_sem, recv_sem
        self.named = {}
        self.pair_of = {origin: n for n, pair in enumerate(PAIRED) for origin in pair}

    def tile_of(self, dx, dz, core):
        x, z, _ = self.at
        return ((x + dx + 4) % 4 * 4 + (z + dz + 4) % 4) * 2 + core

    def copy(self, number, origin, parts, target):
        block = self.buffer.at[self.tile_of(origin[0], origin[1], self.at[2]), parts[0] : parts[1]]
        return pltpu.make_async_remote_copy(
            src_ref=block,
            dst_ref=block,
            send_sem=self.send_sem,
            recv_sem=self.recv_sem.at[number],
            device_id={"tile": target},
            device_id_type=MESH,
        )

    def number(self, name):
        return self.named.setdefault(name, len(self.named))

    def send(self, name, origin, parts, step):
        self.copy(self.number(name), origin, parts, self.tile_of(step[0], step[1], self.at[2])).start()

    def share(self, origin, parts):
        number = RING_COPIES + self.pair_of[origin]
        self.copy(number, origin, parts, self.tile_of(0, 0, 1 - self.at[2])).start()

    def arrive(self, name, origin, parts):
        self.copy(self.number(name), origin, parts, self.tile_of(0, 0, 1 - self.at[2])).wait_recv()

    def shared(self, pair):
        whole = self.buffer.at[0:2]
        pltpu.make_async_copy(whole, whole, self.recv_sem.at[RING_COPIES + pair]).wait()

    def settle(self):
        whole = self.buffer.at[0 : TILES - 1]
        pltpu.make_async_copy(whole, whole, self.send_sem).wait()


def gather_steps(ring):
    def place(family, first, second):
        return (first, second) if family == 0 else (second, first)

    def both(family):
        return (2 * family, 2 * family + 2)

    def part(family, which):
        return (2 * family + which, 2 * family + which + 1)

    def begin():
        for family in range(2):
            ring.send((family, "f", 1), (0, 0), both(family), place(family, 1, 0))
            ring.send((family, "f", -1), (0, 0), both(family), place(family, -1, 0))
        for family in range(2):
            for step in (1, -1):
                ring.send((family, "s", 0, step), (0, 0), both(family), place(family, 0, step))
        for family in range(2):
            ring.share((0, 0), both(family))

    def spread_first(family, k):
        for step in (1, -1):
            ring.send((family, "s", k, step), place(family, k, 0), both(family), place(family, 0, step))
        ring.share(place(family, k, 0), both(family))

    def near():
        for family in range(2):
            for step in (1, -1):
                origin = place(family, -step, 0)
                ring.arrive((family, "f", step), origin, both(family))
                ring.send((family, "g", step), origin, part(family, 0 if step == 1 else 1), place(family, step, 0))
        for family in range(2):
            for k in (-1, 1):
                spread_first(family, k)

    def far():
        for family in range(2):
            for step in (1, -1):
                ring.arrive((family, "g", step), place(family, 2, 0), part(family, 0 if step == 1 else 1))
            spread_first(family, 2)

    def second(k):
        def run():
            for family in range(2):
                for step in (1, -1):
                    origin = place(family, k, -step)
                    ring.arrive((family, "s", k, step), origin, both(family))
                    ring.send((family, "t", k, step), origin, part(family, 0 if step == 1 else 1), place(family, 0, step))
                    ring.share(origin, both(family))

        return run

    def last(k):
        def run():
            for family in range(2):
                for step in (1, -1):
                    ring.arrive((family, "t", k, step), place(family, k, 2), part(family, 0 if step == 1 else 1))
                ring.share(place(family, k, 2), both(family))

        return run

    steps = {"begin": begin, "near": near, "far": far}
    for k in (0, -1, 1, 2):
        steps["second", k] = second(k)
        steps["last", k] = last(k)
    return steps


KC = NO * PART_C
JP = NO // 2
JP_STEP = 4
FAR = 72
BLOCK = PART_J * PART_J
OUT_ROWS = OWN + BLOCK + FAR + 16


def contract_body(
    occ_s, virt_s, virt_ref, t_hbm, v_hbm, w_hbm, out_ref,
    t_ref, t_all, w_all, v_all, t_sem, v_sem, w_sem, send_sem, recv_sem,
    index_ref, column_ref, rows_ref, perm_ref, x_all, slot_ref, right_ref, cut_one_ref,
    ladder_ref, cut_ref, left_ref, c_index_ref, total_ref, both_a, both_b, z_ref, *exchange_refs,
):
    tile = lax.axis_index("tile")
    grp = lax.axis_index("grp")
    first_a = tile * PART_A
    first_c = grp * PART_C
    own_ref = out_ref.at[0:OWN]
    near_ref = out_ref.at[OWN : OWN + BLOCK]
    far_ref = out_ref.at[OWN + BLOCK : OWN + BLOCK + FAR]
    t_copy = pltpu.make_async_copy(t_hbm, t_ref, t_sem)
    t_copy.start()
    for n in range(2):
        pltpu.make_async_copy(v_hbm.at[:, :, n], v_all.at[n], v_sem).start()

    ring = Ring(t_all, send_sem, recv_sem)
    steps = gather_steps(ring)
    core = ring.at[2]
    barrier = pltpu.get_barrier_semaphore()
    for target in (
        ring.tile_of(1, 0, core), ring.tile_of(-1, 0, core), ring.tile_of(0, 1, core),
        ring.tile_of(0, -1, core), ring.tile_of(0, 0, 1 - core),
    ):
        pl.semaphore_signal(barrier, inc=1, device_id={"tile": target}, device_id_type=MESH)
    for d in range(1, GRPS):
        pl.semaphore_signal(barrier, inc=1, device_id={"grp": (grp + d) % GRPS}, device_id_type=MESH)

    col, table, rank, rank_col = slot_tables(virt_ref[...])
    column_ref[...] = col
    out_ref[OUT_ROWS - 16 : OUT_ROWS - 8] = table.astype(F32)
    out_ref[OUT_ROWS - 8 : OUT_ROWS] = rank.astype(F32)
    c_col = column_ref[pl.ds(pl.multiple_of(first_c, PART_C), PART_C)]
    for irrep in range(IRREPS):
        index_ref[irrep] = pick_rows(table, c_col ^ irrep)
    t_copy.wait()
    pack_rows(occ_s, t_ref, index_ref, rows_ref, t_all, tile)
    pl.semaphore_wait(barrier, 8)
    steps["begin"]()

    virt8 = jnp.broadcast_to(virt_ref[...], (8, NV))
    repeat = iota((NV, 2 * NV), 1) // 2 == iota((NV, 2 * NV), 0)
    irrep_row = spread(virt8, repeat)[0:1]
    rank_row = spread(rank, repeat)[0:1]
    at = iota((2 * IRREPS * SLOTS, 2 * NV), 0)
    par = iota((2 * IRREPS * SLOTS, 2 * NV), 1) % 2
    wanted = (irrep_row == (at // SLOTS) % IRREPS) & (rank_row == at % SLOTS) & (par == at // (IRREPS * SLOTS))
    perm_ref[...] = jnp.where(wanted, 1.0, 0.0).astype(BF16)

    flat_v = v_all.reshape(2 * PART_C * 2 * NV, NV)

    def sort_rows(c, carry):
        right = jnp.concatenate(
            [flat_v[pl.ds(pl.multiple_of((p * PART_C + c) * 2 * NV, 2 * NV), 2 * NV)] for p in range(2)], axis=1
        )
        ordered = jnp.dot(perm_ref[...], right, preferred_element_type=F32).astype(BF16)
        x_all[c] = ordered.reshape(2, IRREPS, SLOTS, 2 * NV)
        return carry

    pltpu.make_async_copy(v_all, v_all, v_sem).wait()
    for n in range(JP):
        pltpu.make_async_copy(w_hbm.at[:, n], w_all.at[n], w_sem).start()
    lax.fori_loop(0, PART_C // 4, sort_rows, 0, unroll=8)
    steps["near"]()
    lax.fori_loop(PART_C // 4, PART_C // 2, sort_rows, 0, unroll=8)
    steps["far"]()
    lax.fori_loop(PART_C // 2, PART_C, sort_rows, 0, unroll=8)
    lane = iota((NV, NV), 1)
    of_a = iota((NV, NV), 0) == first_a + lane // SLOTS
    a_row = spread(virt8, of_a)[0:1]
    mixed = jnp.where(rank_col == lane % SLOTS, col ^ a_row, -1)
    for p in range(4):
        a = 2 * (p % 2) + p // 2
        mine = jnp.where(lane // SLOTS == a, mixed, -1)
        for irrep in range(IRREPS):
            slot_ref[irrep, p * NV : (p + 1) * NV] = jnp.where(mine == irrep, 1.0, 0.0).astype(BF16)

    def pick_slots(pair, carry):
        for odd in range(2):
            irrep = 2 * pair + odd
            for q in range(4):
                blocks = []
                for m in range(8):
                    c = 8 * q + m
                    which = virt_s[first_c + c] ^ irrep
                    blocks.append(jnp.concatenate([x_all[c, 0, which], x_all[c, 1, which]], axis=1))
                got = jnp.dot(jnp.concatenate(blocks, axis=0), slot_ref[irrep], preferred_element_type=F32).astype(BF16)
                for m in range(8):
                    start = m * NV + q * SLOTS
                    right_ref[pair, start : start + SLOTS, odd * NV : (odd + 1) * NV] = got[m * SLOTS : (m + 1) * SLOTS]
        return carry

    lax.fori_loop(0, 2, pick_slots, 0)
    steps["second", 0]()
    lax.fori_loop(2, 4, pick_slots, 0)
    steps["second", -1]()

    occ_col = occupied_column(occ_s, 0, NO)
    subd = iota((NV, 2 * NV), 0)
    laned = iota((NV, 2 * NV), 1)
    of_a2 = subd == first_a + laned // (2 * PART_C)
    of_c2 = subd == first_c + (laned // 2) % PART_C
    a_irrep = spread(virt8, of_a2)
    ac_irrep = (a_irrep ^ spread(virt8, of_c2))[0:1]
    a_rank = spread(rank, of_a2)[0:1]
    deep = (PART_C * SLOTS, 2 * NV)
    row_at = iota(deep, 0)
    lane_at = iota(deep, 1)
    c_at = 8 * ((row_at % NV) // SLOTS) + row_at // NV
    wanted = (c_at == (lane_at // 2) % PART_C) & (lane_at % 2 == 0) & (a_rank == row_at % SLOTS)
    cut_one_ref[...] = jnp.where(wanted, 1.0, 0.0).astype(BF16)
    for a in range(PART_A):
        base = occ_col ^ a_irrep[0:1, 2 * a * PART_C : 2 * a * PART_C + 1]
        for irrep in range(IRREPS):
            c_index_ref[irrep, a * NO : (a + 1) * NO] = pick_rows(table, base ^ irrep)

    each = 2 * ROWS

    def ladder_pair(number):
        origins = PAIRED[number]
        ring.shared(number)
        chips = [ring.tile_of(dx, dz, 0) // 2 for dx, dz in origins]
        slabs = [t_all[pl.ds(2 * chip, 2)].astype(F32) for chip in chips]
        planes = [
            jnp.concatenate(
                [got[:, m // 2, :, (m % 2) * 8 : (m % 2) * 8 + 8].reshape(each, NV) for got in slabs], axis=0
            ).astype(BF16)
            for m in range(8)
        ]
        left = jnp.concatenate(planes, axis=1)
        pair_irrep = jnp.concatenate([occ_col ^ occ_s[3 * chip + u] for chip in chips for u in range(3)], axis=0)
        total = jnp.zeros((2 * each, NV), F32)
        for pair in range(4):
            both = jnp.dot(left, right_ref[pair], preferred_element_type=F32)
            total = jnp.where(pair_irrep == 2 * pair, both[:, :NV], total)
            total = jnp.where(pair_irrep == 2 * pair + 1, both[:, NV:], total)
        piece = jnp.dot(left, cut_one_ref[...], preferred_element_type=F32)
        for n, chip in enumerate(chips):
            rows = pl.ds(pl.multiple_of(chip * each, each), each)
            part = slice(n * each, (n + 1) * each)
            ladder_ref[rows] = total[part]
            for half in range(2):
                lanes = slice(half * NV, (half + 1) * NV)
                cut_ref[half, rows] = jnp.where(pair_irrep[part] == ac_irrep[:, lanes], piece[part, lanes], 0.0)

    ladder_pair(0)
    steps["second", 1]()
    ladder_pair(1)
    steps["second", 2]()
    ladder_pair(2)
    steps["last", 0]()
    ladder_pair(3)
    steps["last", -1]()
    steps["last", 1]()
    ladder_pair(4)
    steps["last", 2]()
    for number in range(5, 8):
        ladder_pair(number)

    lane48 = iota((NO, NV), 1)
    odd_half = lane48 // (2 * PART_C) == 1

    def left_block(chunk, carry):
        for half in range(2):
            lower = cut_ref[half, pl.ds(2 * chunk, NO, stride=NO)]
            upper = cut_ref[half, pl.ds(2 * chunk + 1, NO, stride=NO)]
            even_a = jnp.where(odd_half, pltpu.roll(upper, 2 * PART_C, 1), lower)
            odd_a = jnp.where(odd_half, upper, pltpu.roll(lower, 2 * PART_C, 1))
            for odd, piece in enumerate((even_a, odd_a)):
                a = 2 * half + odd
                lanes = pl.ds(pl.multiple_of(chunk * NV, NV), NV)
                left_ref[a * NO : (a + 1) * NO, lanes] = piece.astype(BF16)
                left_ref[(PART_A + a) * NO : (PART_A + a + 1) * NO, lanes] = pltpu.roll(piece, 1, 1).astype(BF16)
        return carry

    lax.fori_loop(0, JP, left_block, 0, unroll=4)

    flat = w_all.reshape(JP * 2 * KC, NV)
    span = 2 * NO
    pltpu.make_async_copy(w_all, w_all, w_sem).wait()

    def cycle_product(n, out):
        right = jnp.concatenate(
            [flat[pl.ds(pl.multiple_of((n * JP_STEP + u) * 2 * KC, 2 * KC), 2 * KC)] for u in range(JP_STEP)], axis=1
        )
        out[...] = jnp.dot(left_ref[...], right, preferred_element_type=F32)

    def cycle_place(n, both):
        for u in range(JP_STEP):
            for odd in range(2):
                j = (n * JP_STEP + u) * 2 + odd
                rows = both[odd * PART_A * NO : (odd + 1) * PART_A * NO, u * NV : (u + 1) * NV]
                got = lanes_at(rows, c_index_ref[occ_s[j]])
                value = got[3 * NO :]
                for a in (2, 1, 0):
                    value = jnp.where(lane48 // SLOTS == a, got[a * NO : (a + 1) * NO], value)
                value = value + 0.5 * ladder_ref[pl.ds(j, NO, stride=NO)]
                start = pl.multiple_of(j * span, NO)
                total_ref[pl.ds(start, NO)] = value
                total_ref[pl.ds(start + NO, NO)] = value

    cycle_product(0, both_a)

    def cycle_pair(n, carry):
        cycle_product(2 * n + 1, both_b)
        cycle_place(2 * n, both_a)
        cycle_product(2 * n + 2, both_a)
        cycle_place(2 * n + 1, both_b)
        return carry

    blocks = JP // JP_STEP
    lax.fori_loop(0, blocks // 2 - 1, cycle_pair, 0)
    cycle_product(blocks - 1, both_b)
    cycle_place(blocks - 2, both_a)
    cycle_place(blocks - 1, both_b)
    total_ref[pl.ds(NO * span, TURN * span)] = total_ref[pl.ds(0, TURN * span)]

    def anti(j, carry):
        ahead = total_ref[pl.ds(j * span + j + 1, TURN, stride=1)]
        across = total_ref[pl.ds((j + 1) * span + j, TURN, stride=span)]
        z_ref[j] = ahead - across
        return carry

    lax.fori_loop(0, NO, anti, 0, unroll=4)
    exchange_part(occ_s, virt8, table, rank, z_ref, own_ref, near_ref, far_ref, *exchange_refs)
    ring.settle()


def contract(occ, virt, virt_row, amplitudes, ladder_pairs, cycle_pairs):
    pairs = NO * NO
    half = (PART_J // 2, TURN, NV)
    vmem = pl.BlockSpec(memory_space=pltpu.VMEM)
    smem = pl.BlockSpec(memory_space=pltpu.SMEM)
    hbm = pl.BlockSpec(memory_space=pl.ANY)
    return pl.pallas_call(
        contract_body,
        out_shape=jax.ShapeDtypeStruct((OUT_ROWS, NV), F32),
        in_specs=[smem, smem, vmem, hbm, hbm, hbm],
        out_specs=vmem,
        scratch_shapes=[
            pltpu.VMEM((ROWS, PART_C, NV), BF16),
            pltpu.VMEM((TILES, 4, ROWS // 8, 16, NV), BF16),
            pltpu.VMEM((JP, KC, 2, NV), BF16),
            pltpu.VMEM((2, PART_C, NV, 2, NV), BF16),
            pltpu.SemaphoreType.DMA,
            pltpu.SemaphoreType.DMA,
            pltpu.SemaphoreType.DMA,
            pltpu.SemaphoreType.DMA,
            pltpu.SemaphoreType.DMA((RING_COPIES + len(PAIRED),)),
            pltpu.VMEM((IRREPS, PART_C, NV), I32),
            pltpu.VMEM((NV, NV), I32),
            pltpu.VMEM((ROWS * 8, NV), F32),
            pltpu.VMEM((2 * IRREPS * SLOTS, 2 * NV), BF16),
            pltpu.VMEM((PART_C, 2, IRREPS, SLOTS, 2 * NV), BF16),
            pltpu.VMEM((IRREPS, 4 * NV, NV), BF16),
            pltpu.VMEM((4, PART_C * SLOTS, 2 * NV), BF16),
            pltpu.VMEM((PART_C * SLOTS, 2 * NV), BF16),
            pltpu.VMEM((pairs, NV), F32),
            pltpu.VMEM((2, pairs, NV), F32),
            pltpu.VMEM((2 * PART_A * NO, 2 * KC), BF16),
            pltpu.VMEM((IRREPS, PART_A * NO, NV), I32),
            pltpu.VMEM(((NO + TURN) * 2 * NO, NV), F32),
            pltpu.VMEM((2 * PART_A * NO, JP_STEP * NV), F32),
            pltpu.VMEM((2 * PART_A * NO, JP_STEP * NV), F32),
            pltpu.VMEM((NO, TURN, NV), F32),
            pltpu.VMEM((2,) + half, F32),
            pltpu.VMEM((4,) + half, F32),
            pltpu.VMEM((2,) + half, F32),
            pltpu.VMEM((TILES, SHARE, NV), F32),
            pltpu.VMEM((TILES * PITCH, NV), F32),
            pltpu.VMEM((TILES, SHARE, NV), F32),
            pltpu.VMEM((TILES * PITCH, NV), F32),
            pltpu.VMEM((IRREPS, NV, NV), I32),
            pltpu.VMEM((BLOCK, NV), F32),
            pltpu.VMEM((FAR, NV), F32),
            pltpu.SemaphoreType.DMA((6,)),
            pltpu.SemaphoreType.DMA((6,)),
            pltpu.SemaphoreType.DMA,
            pltpu.SemaphoreType.DMA,
            pltpu.SemaphoreType.DMA,
            pltpu.SemaphoreType.DMA,
            pltpu.SemaphoreType.DMA((2,)),
            pltpu.SemaphoreType.DMA((2,)),
        ],
        compiler_params=pltpu.CompilerParams(
            vmem_limit_bytes=62 * 2**20, collective_id=0, has_side_effects=True
        ),
        name="contract",
    )(occ, virt, virt_row, amplitudes, ladder_pairs, cycle_pairs)


def exchange_part(
    occ_s, virt8, table, rank, z_ref, own_ref, near_ref, far_ref,
    stage_ref, direct_ref, merged_ref, first_ref, first_in, second_ref, second_in,
    index_ref, near_out, far_out, sum_send, sum_recv, a_send, a_recv, b_send, b_recv, f_send, f_recv,
):
    tile = lax.axis_index("tile")
    grp = lax.axis_index("grp")
    up, down, over = (grp + 1) % GRPS, (grp + 3) % GRPS, (grp + 2) % GRPS
    half = PART_J // 2

    def block(owner, part):
        return pl.ds(owner * PART_J + part * half, half)

    def to(axis, target, src, dst, send, recv):
        return pltpu.make_async_remote_copy(
            src_ref=src, dst_ref=dst, send_sem=send, recv_sem=recv,
            device_id={axis: target}, device_id_type=MESH,
        )

    sends = [
        to("grp", up, z_ref.at[block(over, 0)], stage_ref.at[0], sum_send.at[0], sum_recv.at[0]),
        to("grp", down, z_ref.at[block(over, 1)], stage_ref.at[1], sum_send.at[1], sum_recv.at[1]),
        to("grp", up, z_ref.at[block(up, 1)], direct_ref.at[0], sum_send.at[2], sum_recv.at[2]),
        to("grp", down, z_ref.at[block(down, 0)], direct_ref.at[1], sum_send.at[3], sum_recv.at[3]),
        to("grp", up, merged_ref.at[0], direct_ref.at[2], sum_send.at[4], sum_recv.at[4]),
        to("grp", down, merged_ref.at[1], direct_ref.at[3], sum_send.at[5], sum_recv.at[5]),
    ]
    for number in (0, 3, 1):
        sends[number].start()

    sub = iota((NV, NV), 0)
    lane = iota((NV, NV), 1)
    turned = sub == 4 * (lane % SLOTS) + lane // SLOTS
    rank_turned = spread(rank, turned)[0:1]
    irrep_turned = spread(virt8, turned)[0:1]
    irrep_col = column_of(irrep_turned)
    table_turned = (table % 4) * SLOTS + table // 4
    for irrep in range(IRREPS):
        index_ref[irrep] = pick_rows(table_turned, irrep_col ^ irrep)

    def swap(src, dst, send, recv, target):
        to("tile", target, src.at[target], dst.at[pl.ds(pl.multiple_of(tile * PITCH, PITCH), SHARE)], send, recv).start()

    def swapped(dst, sem):
        rows = dst.at[0 : (TILES - 1) * SHARE]
        pltpu.make_async_copy(rows, rows, sem).wait()

    def first_half(part, value):
        own_ref[part * OWN // 2 : (part + 1) * OWN // 2] = value.reshape(OWN // 2, NV)
        near_tiles = TILES // 2
        for u in range(part * near_tiles, (part + 1) * near_tiles):
            first_ref[u] = own_ref[u * SHARE : (u + 1) * SHARE]
        for d in range(near_tiles):
            target = part * near_tiles + (tile + d) % near_tiles
            if d == 0:
                pl.when(tile // near_tiles != part)(
                    functools.partial(swap, first_ref, first_in, a_send, a_recv, target)
                )
            else:
                swap(first_ref, first_in, a_send, a_recv, target)

    sends[0].wait_recv()
    merged_ref[0] = stage_ref[0] + z_ref[block(up, 0)]
    sends[4].start()
    sends[2].start()
    sends[1].wait_recv()
    merged_ref[1] = stage_ref[1] + z_ref[block(down, 1)]
    sends[5].start()
    sends[3].wait_recv()
    sends[4].wait_recv()
    first_half(0, z_ref[block(grp, 0)] + direct_ref[1] + direct_ref[2])
    sends[2].wait_recv()
    sends[5].wait_recv()
    first_half(1, z_ref[block(grp, 1)] + direct_ref[0] + direct_ref[3])
    first_in[pl.ds(pl.multiple_of(tile * PITCH, PITCH), SHARE)] = first_ref[tile]
    swapped(first_in, a_recv)

    quarter = iota((TILES, NV), 1) // SLOTS

    def one(n, carry):
        row = tile * SHARE + n
        j = grp * PART_J + row // TURN
        i = (j + row % TURN + 1) % NO
        irrep = occ_s[i] ^ occ_s[j]
        rows = first_in[pl.ds(n, TILES, stride=PITCH)]
        full = jnp.concatenate(
            [lanes_at(rows, jnp.broadcast_to(rank_turned + a * SLOTS, (TILES, NV))) for a in range(PART_A)], axis=0
        )
        anti = full - full.T
        got = lanes_at(anti, index_ref[irrep])
        value = got[3 * TILES :]
        for a in (2, 1, 0):
            value = jnp.where(quarter == a, got[a * TILES : (a + 1) * TILES], value)
        for t in range(TILES):
            second_ref[t, pl.ds(n, 1)] = value[t : t + 1]
        return carry

    lax.fori_loop(0, SHARE, one, 0, unroll=3)
    second_in[pl.ds(pl.multiple_of(tile * PITCH, PITCH), SHARE)] = second_ref[tile]
    for d in range(1, TILES):
        swap(second_ref, second_in, b_send, b_recv, (tile + d) % TILES)
    swapped(second_in, b_recv)
    for u in range(TILES):
        own_ref[u * SHARE : (u + 1) * SHARE] = second_in[u * PITCH : u * PITCH + SHARE]
    for x in range(PART_J):
        near_out[x * PART_J : (x + 1) * PART_J] = own_ref[x * TURN + 11 - x : x * TURN + 23 - x]
    far_out[FAR - 8 : FAR] = jnp.zeros((8, NV), F32)
    filled = 0
    for y in range(PART_J - 1):
        count = PART_J - 1 - y
        far_out[filled : filled + count] = own_ref[pl.ds((y + 1) * (TURN - 1) + 23 + y, count, stride=TURN - 1)]
        filled += count
    ends = [
        to("grp", up, near_out, near_ref, f_send.at[0], f_recv.at[0]),
        to("grp", over, far_out, far_ref, f_send.at[1], f_recv.at[1]),
    ]
    for copy in ends:
        copy.start()
    for copy in sends:
        copy.wait_send()
    swapped(first_in, a_send)
    swapped(second_in, b_send)
    for copy in ends:
        copy.wait()


def expand_body(occ_s, virt_ref, in_ref, out_ref, rows_ref):
    own_ref = in_ref.at[0:OWN]
    near_ref = in_ref.at[OWN : OWN + BLOCK]
    far_ref = in_ref.at[OWN + BLOCK : OWN + BLOCK + FAR]
    first_a = lax.axis_index("tile") * PART_A
    grp = lax.axis_index("grp")
    first_j = grp * PART_J
    occ_col = occupied_column(occ_s, first_j, NO)
    virt_row = jnp.broadcast_to(virt_ref[...], (NO, NV))
    rank_row = jnp.broadcast_to(in_ref[OUT_ROWS - 8 : OUT_ROWS - 7], (NO, NV)).astype(I32)
    virt8 = jnp.broadcast_to(virt_ref[...], (8, NV))
    a_irrep = spread(virt8, iota((NV, NV), 0) == first_a + iota((NV, NV), 1) // PART_C)
    n = PART_J
    for x in range(n):
        at = rows_ref.at[x]
        at[x : x + 1] = jnp.zeros((1, NV), F32)
        if x < n - 1:
            at[x + 1 : n] = own_ref[x * TURN : x * TURN + n - 1 - x]
        if x > 0:
            at[0:x] = -own_ref[pl.ds(x - 1, x, stride=TURN - 1)]
        at[n : 2 * n] = own_ref[x * TURN + 11 - x : x * TURN + 23 - x]
        at[2 * n : 2 * n + x + 1] = own_ref[x * TURN + 23 - x : x * TURN + 24]
        if x < n - 1:
            filled = x * (n - 1) - x * (x - 1) // 2
            at[2 * n + x + 1 : 3 * n] = -far_ref[filled : filled + n - 1 - x]
        at[3 * n : 4 * n] = -near_ref[pl.ds(x, n, stride=n)]
    for x in range(n):
        rows = rows_ref[x]
        irrep_j = occ_s[first_j + x]
        for a in range(PART_A):
            got = lanes_at(rows, rank_row + a * SLOTS)
            want = virt_row ^ a_irrep[0:1, a * PART_C : a * PART_C + 1] ^ irrep_j
            value = jnp.where(occ_col == want, got, 0.0)
            for b in range(GRPS):
                start = lax.rem(grp + b, GRPS) * (n * n * PART_A) + x * PART_A + a
                out_ref[pl.ds(start, n, stride=n * PART_A)] = value[b * n : (b + 1) * n]


def expand(occ, virt_row, compact):
    vmem = pl.BlockSpec(memory_space=pltpu.VMEM)
    return pl.pallas_call(
        expand_body,
        out_shape=jax.ShapeDtypeStruct((NO * PART_J * PART_A, NV), F32),
        in_specs=[pl.BlockSpec(memory_space=pltpu.SMEM), vmem, vmem],
        out_specs=vmem,
        scratch_shapes=[pltpu.VMEM((PART_J, NO, NV), F32)],
        compiler_params=pltpu.CompilerParams(vmem_limit_bytes=32 * 2**20),
        name="expand",
    )(occ, virt_row, compact)


def shards(amplitudes, ladder_ints, cycle_ints, occ_irrep, virt_irrep):
    virt_row = virt_irrep.reshape(1, NV)
    compact = contract(
        occ_irrep, virt_irrep, virt_row, amplitudes,
        ladder_ints.reshape(PART_C, NV, 2, 2, NV), cycle_ints.reshape(KC, JP, 2, NV),
    )
    return expand(occ_irrep, virt_row, compact).reshape(NO, PART_J, PART_A, NV)


def solution(mesh):
    placed = (
        P("tile", "grp", None),
        P("grp", None, "tile", None),
        P(None, "grp", None, None),
        P(),
        P(),
    )
    return jax.shard_map(
        shards, mesh=mesh, in_specs=placed, out_specs=P(None, "grp", "tile", None), check_vma=False
    )
```

```python
import functools

import jax
import jax.numpy as jnp
from jax import lax
from jax.experimental import pallas as pl
from jax.experimental.pallas import tpu as pltpu
from jax.sharding import PartitionSpec as P

NO = 48
NV = 128
SLOTS = 32
PART_C = 32
PART_A = 4
PART_J = 12
TILES = 32
GRPS = 4
ROWS = 72
TURN = 24
OWN = PART_J * TURN
SHARE = OWN // TILES
PITCH = 16
MESH = pl.DeviceIdType.MESH
IRREPS = 8
F32 = jnp.float32
BF16 = jnp.bfloat16
I32 = jnp.int32


def iota(shape, axis):
    return lax.broadcasted_iota(I32, shape, axis)


def lanes_at(values, index):
    return jnp.take_along_axis(values, index, axis=1, mode="promise_in_bounds")


def spread(selector, values):
    return jnp.dot(selector.astype(BF16), values.astype(BF16), preferred_element_type=F32).astype(I32)


def pick_rows(table, which):
    picked = jnp.broadcast_to(table[0:1], which.shape)
    for irrep in range(1, IRREPS):
        picked = jnp.where(which == irrep, jnp.broadcast_to(table[irrep : irrep + 1], which.shape), picked)
    return picked


def column_of(virt_row):
    return jnp.broadcast_to(virt_row, (NV, NV)).astype(F32).T.astype(I32)


def occupied_column(occ_s, first, rows):
    sub = iota((rows, NV), 0)
    column = jnp.zeros((rows, NV), I32)
    for i in range(rows):
        at = i if isinstance(first, int) else lax.rem(first + i, NO)
        column = jnp.where(sub == i, occ_s[at], column)
    return column


def slot_tables(virt_row):
    row = jnp.broadcast_to(virt_row, (NV, NV))
    col = column_of(virt_row)
    sub = iota((NV, NV), 0)
    lane = iota((NV, NV), 1)
    same = row == col
    rank_col = jnp.sum(jnp.where(same & (lane < sub), 1.0, 0.0), axis=1, keepdims=True)
    rank_row = jnp.sum(jnp.where(same & (sub < lane), 1.0, 0.0), axis=0, keepdims=True)
    hit = jnp.broadcast_to(rank_col, (NV, NV)).astype(I32) == lane % SLOTS
    subf = sub.astype(F32)
    entries = [
        jnp.sum(jnp.where(hit & (col == irrep), subf, 0.0), axis=0, keepdims=True)
        for irrep in range(IRREPS)
    ]
    table = jnp.concatenate(entries, axis=0).astype(I32)
    rank_col = jnp.broadcast_to(rank_col, (NV, NV)).astype(I32)
    return col, table, jnp.broadcast_to(rank_row, (8, NV)).astype(I32), rank_col


def pack_rows(occ_s, t_ref, index_ref, rows_ref, out_ref, me):
    first = lax.axis_index("tile") * ROWS
    quarter = iota((8, NV), 1) // SLOTS

    def one_row(r, carry):
        pair = first + r
        irrep = occ_s[pair // NO] ^ occ_s[pair % NO]
        got = lanes_at(t_ref[r].astype(F32), index_ref[irrep])
        row = got[24:32]
        for q in (2, 1, 0):
            row = jnp.where(quarter == q, got[8 * q : 8 * q + 8], row)
        rows_ref[pl.ds(pl.multiple_of(r * 8, 8), 8)] = row
        return carry

    lax.fori_loop(0, ROWS, one_row, 0, unroll=8)
    for block in range(ROWS // 8):
        for half in range(4):
            pair_of = [
                rows_ref[pl.ds(block * 64 + 2 * half + odd, 8, stride=8)] for odd in range(2)
            ]
            out_ref[me, half, block] = jnp.concatenate(pair_of, axis=0).astype(BF16)


PAIRED = (
    ((0, 0), (1, 0)), ((-1, 0), (0, 1)), ((0, -1), (-1, -1)), ((1, 1), (-1, 1)),
    ((1, -1), (0, 2)), ((2, 0), (1, 2)), ((-1, 2), (2, 1)), ((2, -1), (2, 2)),
)
RING_COPIES = 38


class Ring:
    def __init__(self, t_all, send_sem, recv_sem):
        tile = lax.axis_index("tile")
        self.at = (tile // 8, (tile // 2) % 4, tile % 2)
        self.buffer, self.send_sem, self.recv_sem = t_all, send_sem, recv_sem
        self.named = {}
        self.pair_of = {origin: n for n, pair in enumerate(PAIRED) for origin in pair}

    def tile_of(self, dx, dz, core):
        x, z, _ = self.at
        return ((x + dx + 4) % 4 * 4 + (z + dz + 4) % 4) * 2 + core

    def copy(self, number, origin, parts, target):
        block = self.buffer.at[self.tile_of(origin[0], origin[1], self.at[2]), parts[0] : parts[1]]
        return pltpu.make_async_remote_copy(
            src_ref=block,
            dst_ref=block,
            send_sem=self.send_sem,
            recv_sem=self.recv_sem.at[number],
            device_id={"tile": target},
            device_id_type=MESH,
        )

    def number(self, name):
        return self.named.setdefault(name, len(self.named))

    def send(self, name, origin, parts, step):
        self.copy(self.number(name), origin, parts, self.tile_of(step[0], step[1], self.at[2])).start()

    def share(self, origin, parts):
        number = RING_COPIES + self.pair_of[origin]
        self.copy(number, origin, parts, self.tile_of(0, 0, 1 - self.at[2])).start()

    def arrive(self, name, origin, parts):
        self.copy(self.number(name), origin, parts, self.tile_of(0, 0, 1 - self.at[2])).wait_recv()

    def shared(self, pair):
        whole = self.buffer.at[0:2]
        pltpu.make_async_copy(whole, whole, self.recv_sem.at[RING_COPIES + pair]).wait()

    def settle(self):
        whole = self.buffer.at[0 : TILES - 1]
        pltpu.make_async_copy(whole, whole, self.send_sem).wait()


def gather_steps(ring):
    def place(family, first, second):
        return (first, second) if family == 0 else (second, first)

    def both(family):
        return (2 * family, 2 * family + 2)

    def part(family, which):
        return (2 * family + which, 2 * family + which + 1)

    def begin():
        for family in range(2):
            ring.send((family, "f", 1), (0, 0), both(family), place(family, 1, 0))
            ring.send((family, "f", -1), (0, 0), both(family), place(family, -1, 0))
            ring.send((family, "g"), (0, 0), both(family), place(family, 2, 0))
        for family in range(2):
            for step in (1, -1):
                ring.send((family, "s", 0, step), (0, 0), both(family), place(family, 0, step))
        for family in range(2):
            ring.share((0, 0), both(family))

    def spread_first(family, k):
        for step in (1, -1):
            ring.send((family, "s", k, step), place(family, k, 0), both(family), place(family, 0, step))
        ring.share(place(family, k, 0), both(family))

    def near():
        for family in range(2):
            for step in (1, -1):
                origin = place(family, -step, 0)
                ring.arrive((family, "f", step), origin, both(family))
        for family in range(2):
            for k in (-1, 1):
                spread_first(family, k)

    def far():
        for family in range(2):
            ring.arrive((family, "g"), place(family, 2, 0), both(family))
            spread_first(family, 2)

    def second(k):
        def run():
            for family in range(2):
                for step in (1, -1):
                    origin = place(family, k, -step)
                    ring.arrive((family, "s", k, step), origin, both(family))
                    ring.send((family, "t", k, step), origin, part(family, 0 if step == 1 else 1), place(family, 0, step))
                    ring.share(origin, both(family))

        return run

    def last(k):
        def run():
            for family in range(2):
                for step in (1, -1):
                    ring.arrive((family, "t", k, step), place(family, k, 2), part(family, 0 if step == 1 else 1))
                ring.share(place(family, k, 2), both(family))

        return run

    steps = {"begin": begin, "near": near, "far": far}
    for k in (0, -1, 1, 2):
        steps["second", k] = second(k)
        steps["last", k] = last(k)
    return steps


KC = NO * PART_C
JP = NO // 2
JP_STEP = 4
OUT_ROWS = 3 * OWN + 16
NEAR_TILES = sorted({(TURN * x + 11 + y - x) // SHARE for x in range(PART_J) for y in range(PART_J)})
FAR_TILES = sorted({(TURN * x + 23 + y - x) // SHARE for x in range(PART_J) for y in range(x)})


def contract_body(
    occ_s, virt_s, virt_ref, t_hbm, v_hbm, w_hbm, out_ref,
    t_ref, t_all, w_all, v_all, t_sem, v_sem, w_sem, send_sem, recv_sem,
    index_ref, column_ref, rows_ref, perm_ref, x_all, slot_ref, right_ref, cut_one_ref,
    ladder_ref, cut_ref, left_ref, c_index_ref, total_ref, both_a, both_b, z_ref, *exchange_refs,
):
    tile = lax.axis_index("tile")
    grp = lax.axis_index("grp")
    first_a = tile * PART_A
    first_c = grp * PART_C
    own_ref = out_ref.at[0:OWN]
    near_ref = out_ref.at[OWN : 2 * OWN]
    far_ref = out_ref.at[2 * OWN : 3 * OWN]
    t_copy = pltpu.make_async_copy(t_hbm, t_ref, t_sem)
    t_copy.start()
    for n in range(2):
        pltpu.make_async_copy(v_hbm.at[:, :, n], v_all.at[n], v_sem).start()

    ring = Ring(t_all, send_sem, recv_sem)
    steps = gather_steps(ring)
    core = ring.at[2]
    barrier = pltpu.get_barrier_semaphore()
    for target in (
        ring.tile_of(1, 0, core), ring.tile_of(-1, 0, core), ring.tile_of(0, 1, core),
        ring.tile_of(0, -1, core), ring.tile_of(0, 0, 1 - core), ring.tile_of(2, 0, core), ring.tile_of(0, 2, core),
    ):
        pl.semaphore_signal(barrier, inc=1, device_id={"tile": target}, device_id_type=MESH)
    for d in range(1, GRPS):
        pl.semaphore_signal(barrier, inc=1, device_id={"grp": (grp + d) % GRPS}, device_id_type=MESH)

    col, table, rank, rank_col = slot_tables(virt_ref[...])
    column_ref[...] = col
    out_ref[OUT_ROWS - 16 : OUT_ROWS - 8] = table.astype(F32)
    out_ref[OUT_ROWS - 8 : OUT_ROWS] = rank.astype(F32)
    c_col = column_ref[pl.ds(pl.multiple_of(first_c, PART_C), PART_C)]
    for irrep in range(IRREPS):
        index_ref[irrep] = pick_rows(table, c_col ^ irrep)
    t_copy.wait()
    pack_rows(occ_s, t_ref, index_ref, rows_ref, t_all, tile)
    pl.semaphore_wait(barrier, 10)
    steps["begin"]()

    virt8 = jnp.broadcast_to(virt_ref[...], (8, NV))
    repeat = iota((NV, 2 * NV), 1) // 2 == iota((NV, 2 * NV), 0)
    irrep_row = spread(virt8, repeat)[0:1]
    rank_row = spread(rank, repeat)[0:1]
    at = iota((2 * IRREPS * SLOTS, 2 * NV), 0)
    par = iota((2 * IRREPS * SLOTS, 2 * NV), 1) % 2
    wanted = (irrep_row == (at // SLOTS) % IRREPS) & (rank_row == at % SLOTS) & (par == at // (IRREPS * SLOTS))
    perm_ref[...] = jnp.where(wanted, 1.0, 0.0).astype(BF16)

    flat_v = v_all.reshape(2 * PART_C * 2 * NV, NV)

    def sort_rows(c, carry):
        right = jnp.concatenate(
            [flat_v[pl.ds(pl.multiple_of((p * PART_C + c) * 2 * NV, 2 * NV), 2 * NV)] for p in range(2)], axis=1
        )
        ordered = jnp.dot(perm_ref[...], right, preferred_element_type=F32).astype(BF16)
        x_all[c] = ordered.reshape(2, IRREPS, SLOTS, 2 * NV)
        return carry

    pltpu.make_async_copy(v_all, v_all, v_sem).wait()
    for n in range(JP):
        pltpu.make_async_copy(w_hbm.at[:, n], w_all.at[n], w_sem).start()
    lax.fori_loop(0, PART_C // 4, sort_rows, 0, unroll=8)
    steps["near"]()
    lax.fori_loop(PART_C // 4, PART_C // 2, sort_rows, 0, unroll=8)
    steps["far"]()
    lax.fori_loop(PART_C // 2, PART_C, sort_rows, 0, unroll=8)
    lane = iota((NV, NV), 1)
    of_a = iota((NV, NV), 0) == first_a + lane // SLOTS
    a_row = spread(virt8, of_a)[0:1]
    mixed = jnp.where(rank_col == lane % SLOTS, col ^ a_row, -1)
    for p in range(4):
        a = 2 * (p % 2) + p // 2
        mine = jnp.where(lane // SLOTS == a, mixed, -1)
        for irrep in range(IRREPS):
            slot_ref[irrep, p * NV : (p + 1) * NV] = jnp.where(mine == irrep, 1.0, 0.0).astype(BF16)

    def pick_slots(pair, carry):
        for odd in range(2):
            irrep = 2 * pair + odd
            for q in range(4):
                blocks = []
                for m in range(8):
                    c = 8 * q + m
                    which = virt_s[first_c + c] ^ irrep
                    blocks.append(jnp.concatenate([x_all[c, 0, which], x_all[c, 1, which]], axis=1))
                got = jnp.dot(jnp.concatenate(blocks, axis=0), slot_ref[irrep], preferred_element_type=F32).astype(BF16)
                for m in range(8):
                    start = m * NV + q * SLOTS
                    right_ref[pair, start : start + SLOTS, odd * NV : (odd + 1) * NV] = got[m * SLOTS : (m + 1) * SLOTS]
        return carry

    lax.fori_loop(0, 2, pick_slots, 0)
    steps["second", 0]()
    lax.fori_loop(2, 4, pick_slots, 0)
    steps["second", -1]()

    occ_col = occupied_column(occ_s, 0, NO)
    subd = iota((NV, 2 * NV), 0)
    laned = iota((NV, 2 * NV), 1)
    of_a2 = subd == first_a + laned // (2 * PART_C)
    of_c2 = subd == first_c + (laned // 2) % PART_C
    a_irrep = spread(virt8, of_a2)
    ac_irrep = (a_irrep ^ spread(virt8, of_c2))[0:1]
    a_rank = spread(rank, of_a2)[0:1]
    deep = (PART_C * SLOTS, 2 * NV)
    row_at = iota(deep, 0)
    lane_at = iota(deep, 1)
    c_at = 8 * ((row_at % NV) // SLOTS) + row_at // NV
    wanted = (c_at == (lane_at // 2) % PART_C) & (lane_at % 2 == 0) & (a_rank == row_at % SLOTS)
    cut_one_ref[...] = jnp.where(wanted, 1.0, 0.0).astype(BF16)
    for a in range(PART_A):
        base = occ_col ^ a_irrep[0:1, 2 * a * PART_C : 2 * a * PART_C + 1]
        for irrep in range(IRREPS):
            c_index_ref[irrep, a * NO : (a + 1) * NO] = pick_rows(table, base ^ irrep)

    each = 2 * ROWS

    def ladder_pair(number):
        origins = PAIRED[number]
        ring.shared(number)
        chips = [ring.tile_of(dx, dz, 0) // 2 for dx, dz in origins]
        slabs = [t_all[pl.ds(2 * chip, 2)].astype(F32) for chip in chips]
        planes = [
            jnp.concatenate(
                [got[:, m // 2, :, (m % 2) * 8 : (m % 2) * 8 + 8].reshape(each, NV) for got in slabs], axis=0
            ).astype(BF16)
            for m in range(8)
        ]
        left = jnp.concatenate(planes, axis=1)
        pair_irrep = jnp.concatenate([occ_col ^ occ_s[3 * chip + u] for chip in chips for u in range(3)], axis=0)
        total = jnp.zeros((2 * each, NV), F32)
        for pair in range(4):
            both = jnp.dot(left, right_ref[pair], preferred_element_type=F32)
            total = jnp.where(pair_irrep == 2 * pair, both[:, :NV], total)
            total = jnp.where(pair_irrep == 2 * pair + 1, both[:, NV:], total)
        piece = jnp.dot(left, cut_one_ref[...], preferred_element_type=F32)
        for n, chip in enumerate(chips):
            rows = pl.ds(pl.multiple_of(chip * each, each), each)
            part = slice(n * each, (n + 1) * each)
            ladder_ref[rows] = total[part]
            for half in range(2):
                lanes = slice(half * NV, (half + 1) * NV)
                cut_ref[half, rows] = jnp.where(pair_irrep[part] == ac_irrep[:, lanes], piece[part, lanes], 0.0)

    steps["second", 1]()
    ladder_pair(0)
    steps["second", 2]()
    ladder_pair(1)
    ladder_pair(2)
    steps["last", 0]()
    ladder_pair(3)
    ladder_pair(4)
    steps["last", -1]()
    steps["last", 1]()
    ladder_pair(5)
    steps["last", 2]()
    ladder_pair(6)
    ladder_pair(7)

    lane48 = iota((NO, NV), 1)
    odd_half = lane48 // (2 * PART_C) == 1

    def left_block(chunk, carry):
        for half in range(2):
            lower = cut_ref[half, pl.ds(2 * chunk, NO, stride=NO)]
            upper = cut_ref[half, pl.ds(2 * chunk + 1, NO, stride=NO)]
            even_a = jnp.where(odd_half, pltpu.roll(upper, 2 * PART_C, 1), lower)
            odd_a = jnp.where(odd_half, upper, pltpu.roll(lower, 2 * PART_C, 1))
            for odd, piece in enumerate((even_a, odd_a)):
                a = 2 * half + odd
                lanes = pl.ds(pl.multiple_of(chunk * NV, NV), NV)
                left_ref[a * NO : (a + 1) * NO, lanes] = piece.astype(BF16)
                left_ref[(PART_A + a) * NO : (PART_A + a + 1) * NO, lanes] = pltpu.roll(piece, 1, 1).astype(BF16)
        return carry

    lax.fori_loop(0, JP, left_block, 0, unroll=4)

    flat = w_all.reshape(JP * 2 * KC, NV)
    span = 2 * NO
    pltpu.make_async_copy(w_all, w_all, w_sem).wait()

    def cycle_product(n, out):
        right = jnp.concatenate(
            [flat[pl.ds(pl.multiple_of((n * JP_STEP + u) * 2 * KC, 2 * KC), 2 * KC)] for u in range(JP_STEP)], axis=1
        )
        out[...] = jnp.dot(left_ref[...], right, preferred_element_type=F32)

    def cycle_place(n, both):
        for u in range(JP_STEP):
            for odd in range(2):
                j = (n * JP_STEP + u) * 2 + odd
                rows = both[odd * PART_A * NO : (odd + 1) * PART_A * NO, u * NV : (u + 1) * NV]
                got = lanes_at(rows, c_index_ref[occ_s[j]])
                value = got[3 * NO :]
                for a in (2, 1, 0):
                    value = jnp.where(lane48 // SLOTS == a, got[a * NO : (a + 1) * NO], value)
                value = value + 0.5 * ladder_ref[pl.ds(j, NO, stride=NO)]
                start = pl.multiple_of(j * span, NO)
                total_ref[pl.ds(start, NO)] = value
                total_ref[pl.ds(start + NO, NO)] = value

    cycle_product(0, both_a)

    def cycle_pair(n, carry):
        cycle_product(2 * n + 1, both_b)
        cycle_place(2 * n, both_a)
        cycle_product(2 * n + 2, both_a)
        cycle_place(2 * n + 1, both_b)
        return carry

    blocks = JP // JP_STEP
    lax.fori_loop(0, blocks // 2 - 1, cycle_pair, 0)
    cycle_product(blocks - 1, both_b)
    cycle_place(blocks - 2, both_a)
    cycle_place(blocks - 1, both_b)
    total_ref[pl.ds(NO * span, TURN * span)] = total_ref[pl.ds(0, TURN * span)]

    def anti(j, carry):
        ahead = total_ref[pl.ds(j * span + j + 1, TURN, stride=1)]
        across = total_ref[pl.ds((j + 1) * span + j, TURN, stride=span)]
        z_ref[j] = ahead - across
        return carry

    lax.fori_loop(0, NO, anti, 0, unroll=4)
    exchange_part(occ_s, virt8, table, rank, z_ref, own_ref, near_ref, far_ref, *exchange_refs)
    ring.settle()


def contract(occ, virt, virt_row, amplitudes, ladder_pairs, cycle_pairs):
    pairs = NO * NO
    half = (PART_J // 2, TURN, NV)
    vmem = pl.BlockSpec(memory_space=pltpu.VMEM)
    smem = pl.BlockSpec(memory_space=pltpu.SMEM)
    hbm = pl.BlockSpec(memory_space=pl.ANY)
    return pl.pallas_call(
        contract_body,
        out_shape=jax.ShapeDtypeStruct((OUT_ROWS, NV), F32),
        in_specs=[smem, smem, vmem, hbm, hbm, hbm],
        out_specs=vmem,
        scratch_shapes=[
            pltpu.VMEM((ROWS, PART_C, NV), BF16),
            pltpu.VMEM((TILES, 4, ROWS // 8, 16, NV), BF16),
            pltpu.VMEM((JP, KC, 2, NV), BF16),
            pltpu.VMEM((2, PART_C, NV, 2, NV), BF16),
            pltpu.SemaphoreType.DMA,
            pltpu.SemaphoreType.DMA,
            pltpu.SemaphoreType.DMA,
            pltpu.SemaphoreType.DMA,
            pltpu.SemaphoreType.DMA((RING_COPIES + len(PAIRED),)),
            pltpu.VMEM((IRREPS, PART_C, NV), I32),
            pltpu.VMEM((NV, NV), I32),
            pltpu.VMEM((ROWS * 8, NV), F32),
            pltpu.VMEM((2 * IRREPS * SLOTS, 2 * NV), BF16),
            pltpu.VMEM((PART_C, 2, IRREPS, SLOTS, 2 * NV), BF16),
            pltpu.VMEM((IRREPS, 4 * NV, NV), BF16),
            pltpu.VMEM((4, PART_C * SLOTS, 2 * NV), BF16),
            pltpu.VMEM((PART_C * SLOTS, 2 * NV), BF16),
            pltpu.VMEM((pairs, NV), F32),
            pltpu.VMEM((2, pairs, NV), F32),
            pltpu.VMEM((2 * PART_A * NO, 2 * KC), BF16),
            pltpu.VMEM((IRREPS, PART_A * NO, NV), I32),
            pltpu.VMEM(((NO + TURN) * 2 * NO, NV), F32),
            pltpu.VMEM((2 * PART_A * NO, JP_STEP * NV), F32),
            pltpu.VMEM((2 * PART_A * NO, JP_STEP * NV), F32),
            pltpu.VMEM((NO, TURN, NV), F32),
            pltpu.VMEM((2, 3) + half, F32),
            pltpu.VMEM((TILES, SHARE, NV), F32),
            pltpu.VMEM((TILES * PITCH, NV), F32),
            pltpu.VMEM((TILES, SHARE, NV), F32),
            pltpu.VMEM((TILES * PITCH, NV), F32),
            pltpu.VMEM((IRREPS, NV, NV), I32),
            pltpu.VMEM((TILES * PITCH, NV), F32),
            pltpu.VMEM((TILES * PITCH, NV), F32),
            pltpu.SemaphoreType.DMA((2, 3)),
            pltpu.SemaphoreType.DMA((2, 3)),
            pltpu.SemaphoreType.DMA,
            pltpu.SemaphoreType.DMA,
            pltpu.SemaphoreType.DMA,
            pltpu.SemaphoreType.DMA,
            pltpu.SemaphoreType.DMA((2,)),
            pltpu.SemaphoreType.DMA((2,)),
        ],
        compiler_params=pltpu.CompilerParams(
            vmem_limit_bytes=62 * 2**20, collective_id=0, has_side_effects=True
        ),
        name="contract",
    )(occ, virt, virt_row, amplitudes, ladder_pairs, cycle_pairs)


def exchange_part(
    occ_s, virt8, table, rank, z_ref, own_ref, near_ref, far_ref,
    direct_ref, first_ref, first_in, second_ref, second_in,
    index_ref, near_in, far_in, sum_send, sum_recv, a_send, a_recv, b_send, b_recv, f_send, f_recv,
):
    tile = lax.axis_index("tile")
    grp = lax.axis_index("grp")
    up, down, over = (grp + 1) % GRPS, (grp + 3) % GRPS, (grp + 2) % GRPS
    half = PART_J // 2

    def block(owner, part):
        return pl.ds(owner * PART_J + part * half, half)

    def to(axis, target, src, dst, send, recv):
        return pltpu.make_async_remote_copy(
            src_ref=src, dst_ref=dst, send_sem=send, recv_sem=recv,
            device_id={axis: target}, device_id_type=MESH,
        )

    sends = [
        to("grp", peer, z_ref.at[block(peer, part)], direct_ref.at[part, n], sum_send.at[part, n], sum_recv.at[part, n])
        for part in range(2)
        for n, peer in enumerate((over, up, down))
    ]
    for copy in sends:
        copy.start()

    sub = iota((NV, NV), 0)
    lane = iota((NV, NV), 1)
    turned = sub == 4 * (lane % SLOTS) + lane // SLOTS
    rank_turned = spread(rank, turned)[0:1]
    irrep_turned = spread(virt8, turned)[0:1]
    irrep_col = column_of(irrep_turned)
    table_turned = (table % 4) * SLOTS + table // 4
    for irrep in range(IRREPS):
        index_ref[irrep] = pick_rows(table_turned, irrep_col ^ irrep)

    def swap(src, dst, send, recv, target):
        to("tile", target, src.at[target], dst.at[pl.ds(pl.multiple_of(tile * PITCH, PITCH), SHARE)], send, recv).start()

    def swapped(dst, sem):
        rows = dst.at[0 : (TILES - 1) * SHARE]
        pltpu.make_async_copy(rows, rows, sem).wait()

    def first_half(part, value):
        own_ref[part * OWN // 2 : (part + 1) * OWN // 2] = value.reshape(OWN // 2, NV)
        near_tiles = TILES // 2
        for u in range(part * near_tiles, (part + 1) * near_tiles):
            first_ref[u] = own_ref[u * SHARE : (u + 1) * SHARE]
        for d in range(near_tiles):
            target = part * near_tiles + (tile + d) % near_tiles
            if d == 0:
                pl.when(tile // near_tiles != part)(
                    functools.partial(swap, first_ref, first_in, a_send, a_recv, target)
                )
            else:
                swap(first_ref, first_in, a_send, a_recv, target)

    for part in range(2):
        for copy in sends[3 * part : 3 * part + 3]:
            copy.wait_recv()
        first_half(part, z_ref[block(grp, part)] + direct_ref[part, 0] + direct_ref[part, 1] + direct_ref[part, 2])
    first_in[pl.ds(pl.multiple_of(tile * PITCH, PITCH), SHARE)] = first_ref[tile]
    swapped(first_in, a_recv)

    quarter = iota((TILES, NV), 1) // SLOTS

    def one(n, carry):
        row = tile * SHARE + n
        j = grp * PART_J + row // TURN
        i = (j + row % TURN + 1) % NO
        irrep = occ_s[i] ^ occ_s[j]
        rows = first_in[pl.ds(n, TILES, stride=PITCH)]
        full = jnp.concatenate(
            [lanes_at(rows, jnp.broadcast_to(rank_turned + a * SLOTS, (TILES, NV))) for a in range(PART_A)], axis=0
        )
        anti = full - full.T
        got = lanes_at(anti, index_ref[irrep])
        value = got[3 * TILES :]
        for a in (2, 1, 0):
            value = jnp.where(quarter == a, got[a * TILES : (a + 1) * TILES], value)
        for t in range(TILES):
            second_ref[t, pl.ds(n, 1)] = value[t : t + 1]
        return carry

    lax.fori_loop(0, SHARE, one, 0, unroll=3)
    def forward(dst, number, peer):
        for d in range(TILES):
            target = (tile + d) % TILES
            pltpu.make_async_remote_copy(
                src_ref=second_ref.at[target],
                dst_ref=dst.at[pl.ds(pl.multiple_of(tile * PITCH, PITCH), SHARE)],
                send_sem=f_send.at[number], recv_sem=f_recv.at[number],
                device_id={"tile": target, "grp": peer}, device_id_type=MESH,
            ).start()

    def taken(dst, sem, tiles):
        rows = dst.at[0 : tiles * SHARE]
        pltpu.make_async_copy(rows, rows, sem).wait()

    in_near = functools.reduce(lambda one, two: one | two, [tile == u for u in NEAR_TILES])
    in_far = functools.reduce(lambda one, two: one | two, [tile == u for u in FAR_TILES])
    pl.when(in_far)(lambda: forward(far_in, 1, over))
    pl.when(in_near)(lambda: forward(near_in, 0, up))
    for d in range(1, TILES):
        swap(second_ref, second_in, b_send, b_recv, (tile + d) % TILES)
    second_in[pl.ds(pl.multiple_of(tile * PITCH, PITCH), SHARE)] = second_ref[tile]
    swapped(second_in, b_recv)
    for u in range(TILES):
        own_ref[u * SHARE : (u + 1) * SHARE] = second_in[u * PITCH : u * PITCH + SHARE]
    taken(near_in, f_recv.at[0], len(NEAR_TILES))
    for u in NEAR_TILES:
        near_ref[u * SHARE : (u + 1) * SHARE] = near_in[u * PITCH : u * PITCH + SHARE]
    taken(far_in, f_recv.at[1], len(FAR_TILES))
    for u in FAR_TILES:
        far_ref[u * SHARE : (u + 1) * SHARE] = far_in[u * PITCH : u * PITCH + SHARE]
    for copy in sends:
        copy.wait_send()
    swapped(first_in, a_send)
    swapped(second_in, b_send)
    pl.when(in_near)(lambda: taken(near_in, f_send.at[0], TILES))
    pl.when(in_far)(lambda: taken(far_in, f_send.at[1], TILES))


def expand_body(occ_s, virt_ref, in_ref, out_ref, rows_ref):
    own_ref = in_ref.at[0:OWN]
    near_ref = in_ref.at[OWN : 2 * OWN]
    far_ref = in_ref.at[2 * OWN : 3 * OWN]
    first_a = lax.axis_index("tile") * PART_A
    grp = lax.axis_index("grp")
    first_j = grp * PART_J
    occ_col = occupied_column(occ_s, first_j, NO)
    virt_row = jnp.broadcast_to(virt_ref[...], (NO, NV))
    rank_row = jnp.broadcast_to(in_ref[OUT_ROWS - 8 : OUT_ROWS - 7], (NO, NV)).astype(I32)
    virt8 = jnp.broadcast_to(virt_ref[...], (8, NV))
    a_irrep = spread(virt8, iota((NV, NV), 0) == first_a + iota((NV, NV), 1) // PART_C)
    n = PART_J
    for x in range(n):
        at = rows_ref.at[x]
        at[x : x + 1] = jnp.zeros((1, NV), F32)
        if x < n - 1:
            at[x + 1 : n] = own_ref[x * TURN : x * TURN + n - 1 - x]
        if x > 0:
            at[0:x] = -own_ref[pl.ds(x - 1, x, stride=TURN - 1)]
        at[n : 2 * n] = own_ref[x * TURN + 11 - x : x * TURN + 23 - x]
        at[2 * n : 2 * n + x + 1] = own_ref[x * TURN + 23 - x : x * TURN + 24]
        if x < n - 1:
            start = (TURN - 1) * (x + 1) + 23 + x
            at[2 * n + x + 1 : 3 * n] = -far_ref[pl.ds(start, n - 1 - x, stride=TURN - 1)]
        at[3 * n : 4 * n] = -near_ref[pl.ds(11 + x, n, stride=TURN - 1)]
    for x in range(n):
        rows = rows_ref[x]
        irrep_j = occ_s[first_j + x]
        for a in range(PART_A):
            got = lanes_at(rows, rank_row + a * SLOTS)
            want = virt_row ^ a_irrep[0:1, a * PART_C : a * PART_C + 1] ^ irrep_j
            value = jnp.where(occ_col == want, got, 0.0)
            for b in range(GRPS):
                start = lax.rem(grp + b, GRPS) * (n * n * PART_A) + x * PART_A + a
                out_ref[pl.ds(start, n, stride=n * PART_A)] = value[b * n : (b + 1) * n]


def expand(occ, virt_row, compact):
    vmem = pl.BlockSpec(memory_space=pltpu.VMEM)
    return pl.pallas_call(
        expand_body,
        out_shape=jax.ShapeDtypeStruct((NO * PART_J * PART_A, NV), F32),
        in_specs=[pl.BlockSpec(memory_space=pltpu.SMEM), vmem, vmem],
        out_specs=vmem,
        scratch_shapes=[pltpu.VMEM((PART_J, NO, NV), F32)],
        compiler_params=pltpu.CompilerParams(vmem_limit_bytes=32 * 2**20),
        name="expand",
    )(occ, virt_row, compact)


def shards(amplitudes, ladder_ints, cycle_ints, occ_irrep, virt_irrep):
    virt_row = virt_irrep.reshape(1, NV)
    compact = contract(
        occ_irrep, virt_irrep, virt_row, amplitudes,
        ladder_ints.reshape(PART_C, NV, 2, 2, NV), cycle_ints.reshape(KC, JP, 2, NV),
    )
    return expand(occ_irrep, virt_row, compact).reshape(NO, PART_J, PART_A, NV)


def solution(mesh):
    placed = (
        P("tile", "grp", None),
        P("grp", None, "tile", None),
        P(None, "grp", None, None),
        P(),
        P(),
    )
    return jax.shard_map(
        shards, mesh=mesh, in_specs=placed, out_specs=P(None, "grp", "tile", None), check_vma=False
    )
```

```python
import functools

import jax
import jax.numpy as jnp
from jax import lax
from jax.experimental import pallas as pl
from jax.experimental.pallas import tpu as pltpu
from jax.sharding import PartitionSpec as P

NO = 48
NV = 128
SLOTS = 32
PART_C = 32
PART_A = 4
PART_J = 12
TILES = 32
GRPS = 4
ROWS = 72
TURN = 24
OWN = PART_J * TURN
SHARE = OWN // TILES
PITCH = 16
MESH = pl.DeviceIdType.MESH
IRREPS = 8
F32 = jnp.float32
BF16 = jnp.bfloat16
I32 = jnp.int32


def iota(shape, axis):
    return lax.broadcasted_iota(I32, shape, axis)


def lanes_at(values, index):
    return jnp.take_along_axis(values, index, axis=1, mode="promise_in_bounds")


def spread(selector, values):
    return jnp.dot(selector.astype(BF16), values.astype(BF16), preferred_element_type=F32).astype(I32)


def pick_rows(table, which):
    picked = jnp.broadcast_to(table[0:1], which.shape)
    for irrep in range(1, IRREPS):
        picked = jnp.where(which == irrep, jnp.broadcast_to(table[irrep : irrep + 1], which.shape), picked)
    return picked


def column_of(virt_row):
    return jnp.broadcast_to(virt_row, (NV, NV)).astype(F32).T.astype(I32)


def occupied_column(occ_s, first, rows):
    sub = iota((rows, NV), 0)
    column = jnp.zeros((rows, NV), I32)
    for i in range(rows):
        at = i if isinstance(first, int) else lax.rem(first + i, NO)
        column = jnp.where(sub == i, occ_s[at], column)
    return column


def slot_tables(virt_row):
    row = jnp.broadcast_to(virt_row, (NV, NV))
    col = column_of(virt_row)
    sub = iota((NV, NV), 0)
    lane = iota((NV, NV), 1)
    same = row == col
    rank_col = jnp.sum(jnp.where(same & (lane < sub), 1.0, 0.0), axis=1, keepdims=True)
    rank_row = jnp.sum(jnp.where(same & (sub < lane), 1.0, 0.0), axis=0, keepdims=True)
    hit = jnp.broadcast_to(rank_col, (NV, NV)).astype(I32) == lane % SLOTS
    subf = sub.astype(F32)
    entries = [
        jnp.sum(jnp.where(hit & (col == irrep), subf, 0.0), axis=0, keepdims=True)
        for irrep in range(IRREPS)
    ]
    table = jnp.concatenate(entries, axis=0).astype(I32)
    rank_col = jnp.broadcast_to(rank_col, (NV, NV)).astype(I32)
    return col, table, jnp.broadcast_to(rank_row, (8, NV)).astype(I32), rank_col


def pack_rows(occ_s, t_ref, index_ref, rows_ref, out_ref, me):
    first = lax.axis_index("tile") * ROWS
    quarter = iota((8, NV), 1) // SLOTS

    def one_row(r, carry):
        pair = first + r
        irrep = occ_s[pair // NO] ^ occ_s[pair % NO]
        got = lanes_at(t_ref[r].astype(F32), index_ref[irrep])
        row = got[24:32]
        for q in (2, 1, 0):
            row = jnp.where(quarter == q, got[8 * q : 8 * q + 8], row)
        rows_ref[pl.ds(pl.multiple_of(r * 8, 8), 8)] = row
        return carry

    lax.fori_loop(0, ROWS, one_row, 0, unroll=8)
    for block in range(ROWS // 8):
        for half in range(4):
            pair_of = [
                rows_ref[pl.ds(block * 64 + 2 * half + odd, 8, stride=8)] for odd in range(2)
            ]
            out_ref[me, half, block] = jnp.concatenate(pair_of, axis=0).astype(BF16)


PAIRED = (
    ((0, 0), (1, 0)), ((-1, 0), (0, 1)), ((0, -1), (-1, -1)), ((1, 1), (-1, 1)),
    ((1, -1), (0, 2)), ((2, 0), (1, 2)), ((-1, 2), (2, 1)), ((2, -1), (2, 2)),
)
RING_COPIES = 38


class Ring:
    def __init__(self, t_all, send_sem, recv_sem):
        tile = lax.axis_index("tile")
        self.at = (tile // 8, (tile // 2) % 4, tile % 2)
        self.buffer, self.send_sem, self.recv_sem = t_all, send_sem, recv_sem
        self.named = {}
        self.pair_of = {origin: n for n, pair in enumerate(PAIRED) for origin in pair}

    def tile_of(self, dx, dz, core):
        x, z, _ = self.at
        return ((x + dx + 4) % 4 * 4 + (z + dz + 4) % 4) * 2 + core

    def copy(self, number, origin, parts, target):
        block = self.buffer.at[self.tile_of(origin[0], origin[1], self.at[2]), parts[0] : parts[1]]
        return pltpu.make_async_remote_copy(
            src_ref=block,
            dst_ref=block,
            send_sem=self.send_sem,
            recv_sem=self.recv_sem.at[number],
            device_id={"tile": target},
            device_id_type=MESH,
        )

    def number(self, name):
        return self.named.setdefault(name, len(self.named))

    def send(self, name, origin, parts, step):
        self.copy(self.number(name), origin, parts, self.tile_of(step[0], step[1], self.at[2])).start()

    def share(self, origin, parts):
        number = RING_COPIES + self.pair_of[origin]
        self.copy(number, origin, parts, self.tile_of(0, 0, 1 - self.at[2])).start()

    def arrive(self, name, origin, parts):
        self.copy(self.number(name), origin, parts, self.tile_of(0, 0, 1 - self.at[2])).wait_recv()

    def shared(self, pair):
        whole = self.buffer.at[0:2]
        pltpu.make_async_copy(whole, whole, self.recv_sem.at[RING_COPIES + pair]).wait()

    def settle(self):
        whole = self.buffer.at[0 : TILES - 1]
        pltpu.make_async_copy(whole, whole, self.send_sem).wait()


def gather_steps(ring):
    def place(family, first, second):
        return (first, second) if family == 0 else (second, first)

    def both(family):
        return (2 * family, 2 * family + 2)

    def part(family, which):
        return (2 * family + which, 2 * family + which + 1)

    def begin():
        for family in range(2):
            ring.send((family, "f", 1), (0, 0), both(family), place(family, 1, 0))
            ring.send((family, "f", -1), (0, 0), both(family), place(family, -1, 0))
            ring.send((family, "g"), (0, 0), both(family), place(family, 2, 0))
        for family in range(2):
            for step in (1, -1):
                ring.send((family, "s", 0, step), (0, 0), both(family), place(family, 0, step))
        for family in range(2):
            ring.share((0, 0), both(family))

    def spread_first(family, k):
        for step in (1, -1):
            ring.send((family, "s", k, step), place(family, k, 0), both(family), place(family, 0, step))
        ring.share(place(family, k, 0), both(family))

    def near():
        for family in range(2):
            for step in (1, -1):
                origin = place(family, -step, 0)
                ring.arrive((family, "f", step), origin, both(family))
        for family in range(2):
            for k in (-1, 1):
                spread_first(family, k)

    def far():
        for family in range(2):
            ring.arrive((family, "g"), place(family, 2, 0), both(family))
            spread_first(family, 2)

    def second(k):
        def run():
            for family in range(2):
                for step in (1, -1):
                    origin = place(family, k, -step)
                    ring.arrive((family, "s", k, step), origin, both(family))
                    ring.send((family, "t", k, step), origin, part(family, 0 if step == 1 else 1), place(family, 0, step))
                    ring.share(origin, both(family))

        return run

    def last(k):
        def run():
            for family in range(2):
                for step in (1, -1):
                    ring.arrive((family, "t", k, step), place(family, k, 2), part(family, 0 if step == 1 else 1))
                ring.share(place(family, k, 2), both(family))

        return run

    steps = {"begin": begin, "near": near, "far": far}
    for k in (0, -1, 1, 2):
        steps["second", k] = second(k)
        steps["last", k] = last(k)
    return steps


KC = NO * PART_C
JP = NO // 2
JP_STEP = 4
OUT_ROWS = 3 * OWN + 16
NEAR_TILES = sorted({(TURN * x + 11 + y - x) // SHARE for x in range(PART_J) for y in range(PART_J)})
FAR_TILES = sorted({(TURN * x + 23 + y - x) // SHARE for x in range(PART_J) for y in range(x)})


def contract_body(
    occ_s, virt_s, virt_ref, t_hbm, v_hbm, w_hbm, out_ref,
    t_ref, t_all, w_all, v_all, t_sem, v_sem, w_sem, send_sem, recv_sem,
    index_ref, column_ref, rows_ref, perm_ref, x_all, slot_ref, right_ref, cut_one_ref,
    ladder_ref, cut_ref, left_ref, c_index_ref, total_ref, both_a, both_b, z_ref, *exchange_refs,
):
    tile = lax.axis_index("tile")
    grp = lax.axis_index("grp")
    first_a = tile * PART_A
    first_c = grp * PART_C
    own_ref = out_ref.at[0:OWN]
    near_ref = out_ref.at[OWN : 2 * OWN]
    far_ref = out_ref.at[2 * OWN : 3 * OWN]
    t_copy = pltpu.make_async_copy(t_hbm, t_ref, t_sem)
    t_copy.start()
    for n in range(2):
        pltpu.make_async_copy(v_hbm.at[:, :, n], v_all.at[n], v_sem).start()

    ring = Ring(t_all, send_sem, recv_sem)
    steps = gather_steps(ring)
    core = ring.at[2]
    barrier = pltpu.get_barrier_semaphore()
    for target in (
        ring.tile_of(1, 0, core), ring.tile_of(-1, 0, core), ring.tile_of(0, 1, core),
        ring.tile_of(0, -1, core), ring.tile_of(0, 0, 1 - core), ring.tile_of(2, 0, core), ring.tile_of(0, 2, core),
    ):
        pl.semaphore_signal(barrier, inc=1, device_id={"tile": target}, device_id_type=MESH)
    for d in range(1, GRPS):
        pl.semaphore_signal(barrier, inc=1, device_id={"grp": (grp + d) % GRPS}, device_id_type=MESH)

    col, table, rank, rank_col = slot_tables(virt_ref[...])
    column_ref[...] = col
    out_ref[OUT_ROWS - 16 : OUT_ROWS - 8] = table.astype(F32)
    out_ref[OUT_ROWS - 8 : OUT_ROWS] = rank.astype(F32)
    c_col = column_ref[pl.ds(pl.multiple_of(first_c, PART_C), PART_C)]
    for irrep in range(IRREPS):
        index_ref[irrep] = pick_rows(table, c_col ^ irrep)
    t_copy.wait()
    pack_rows(occ_s, t_ref, index_ref, rows_ref, t_all, tile)
    pl.semaphore_wait(barrier, 10)
    steps["begin"]()

    virt8 = jnp.broadcast_to(virt_ref[...], (8, NV))
    repeat = iota((NV, 2 * NV), 1) // 2 == iota((NV, 2 * NV), 0)
    irrep_row = spread(virt8, repeat)[0:1]
    rank_row = spread(rank, repeat)[0:1]
    at = iota((2 * IRREPS * SLOTS, 2 * NV), 0)
    par = iota((2 * IRREPS * SLOTS, 2 * NV), 1) % 2
    wanted = (irrep_row == (at // SLOTS) % IRREPS) & (rank_row == at % SLOTS) & (par == at // (IRREPS * SLOTS))
    perm_ref[...] = jnp.where(wanted, 1.0, 0.0).astype(BF16)

    flat_v = v_all.reshape(2 * PART_C * 2 * NV, NV)

    def sort_rows(c, carry):
        right = jnp.concatenate(
            [flat_v[pl.ds(pl.multiple_of((p * PART_C + c) * 2 * NV, 2 * NV), 2 * NV)] for p in range(2)], axis=1
        )
        ordered = jnp.dot(perm_ref[...], right, preferred_element_type=F32).astype(BF16)
        x_all[c] = ordered.reshape(2, IRREPS, SLOTS, 2 * NV)
        return carry

    pltpu.make_async_copy(v_all, v_all, v_sem).wait()
    for n in range(JP):
        pltpu.make_async_copy(w_hbm.at[:, n], w_all.at[n], w_sem).start()
    lax.fori_loop(0, PART_C // 4, sort_rows, 0, unroll=8)
    steps["near"]()
    lax.fori_loop(PART_C // 4, PART_C // 2, sort_rows, 0, unroll=8)
    steps["far"]()
    lax.fori_loop(PART_C // 2, PART_C, sort_rows, 0, unroll=8)
    lane = iota((NV, NV), 1)
    of_a = iota((NV, NV), 0) == first_a + lane // SLOTS
    a_row = spread(virt8, of_a)[0:1]
    mixed = jnp.where(rank_col == lane % SLOTS, col ^ a_row, -1)
    for p in range(4):
        a = 2 * (p % 2) + p // 2
        mine = jnp.where(lane // SLOTS == a, mixed, -1)
        for irrep in range(IRREPS):
            slot_ref[irrep, p * NV : (p + 1) * NV] = jnp.where(mine == irrep, 1.0, 0.0).astype(BF16)

    def pick_slots(pair, carry):
        for odd in range(2):
            irrep = 2 * pair + odd
            for q in range(4):
                blocks = []
                for m in range(8):
                    c = 8 * q + m
                    which = virt_s[first_c + c] ^ irrep
                    blocks.append(jnp.concatenate([x_all[c, 0, which], x_all[c, 1, which]], axis=1))
                got = jnp.dot(jnp.concatenate(blocks, axis=0), slot_ref[irrep], preferred_element_type=F32).astype(BF16)
                for m in range(8):
                    start = m * NV + q * SLOTS
                    right_ref[pair, start : start + SLOTS, odd * NV : (odd + 1) * NV] = got[m * SLOTS : (m + 1) * SLOTS]
        return carry

    lax.fori_loop(0, 2, pick_slots, 0)
    steps["second", 0]()
    lax.fori_loop(2, 4, pick_slots, 0)
    steps["second", -1]()

    occ_col = occupied_column(occ_s, 0, NO)
    subd = iota((NV, 2 * NV), 0)
    laned = iota((NV, 2 * NV), 1)
    of_a2 = subd == first_a + laned // (2 * PART_C)
    of_c2 = subd == first_c + (laned // 2) % PART_C
    a_irrep = spread(virt8, of_a2)
    ac_irrep = (a_irrep ^ spread(virt8, of_c2))[0:1]
    a_rank = spread(rank, of_a2)[0:1]
    deep = (PART_C * SLOTS, 2 * NV)
    row_at = iota(deep, 0)
    lane_at = iota(deep, 1)
    c_at = 8 * ((row_at % NV) // SLOTS) + row_at // NV
    wanted = (c_at == (lane_at // 2) % PART_C) & (lane_at % 2 == 0) & (a_rank == row_at % SLOTS)
    cut_one_ref[...] = jnp.where(wanted, 1.0, 0.0).astype(BF16)
    for a in range(PART_A):
        base = occ_col ^ a_irrep[0:1, 2 * a * PART_C : 2 * a * PART_C + 1]
        for irrep in range(IRREPS):
            c_index_ref[irrep, a * NO : (a + 1) * NO] = pick_rows(table, base ^ irrep)

    each = 2 * ROWS

    def ladder_pair(number):
        origins = PAIRED[number]
        ring.shared(number)
        chips = [ring.tile_of(dx, dz, 0) // 2 for dx, dz in origins]
        slabs = [t_all[pl.ds(2 * chip, 2)].astype(F32) for chip in chips]
        planes = [
            jnp.concatenate(
                [got[:, m // 2, :, (m % 2) * 8 : (m % 2) * 8 + 8].reshape(each, NV) for got in slabs], axis=0
            ).astype(BF16)
            for m in range(8)
        ]
        left = jnp.concatenate(planes, axis=1)
        pair_irrep = jnp.concatenate([occ_col ^ occ_s[3 * chip + u] for chip in chips for u in range(3)], axis=0)
        total = jnp.zeros((2 * each, NV), F32)
        for pair in range(4):
            both = jnp.dot(left, right_ref[pair], preferred_element_type=F32)
            total = jnp.where(pair_irrep == 2 * pair, both[:, :NV], total)
            total = jnp.where(pair_irrep == 2 * pair + 1, both[:, NV:], total)
        piece = jnp.dot(left, cut_one_ref[...], preferred_element_type=F32)
        for n, chip in enumerate(chips):
            rows = pl.ds(pl.multiple_of(chip * each, each), each)
            part = slice(n * each, (n + 1) * each)
            ladder_ref[rows] = total[part]
            for half in range(2):
                lanes = slice(half * NV, (half + 1) * NV)
                cut_ref[half, rows] = jnp.where(pair_irrep[part] == ac_irrep[:, lanes], piece[part, lanes], 0.0)

    steps["second", 1]()
    ladder_pair(0)
    steps["second", 2]()
    ladder_pair(1)
    ladder_pair(2)
    steps["last", 0]()
    ladder_pair(3)
    ladder_pair(4)
    steps["last", -1]()
    steps["last", 1]()
    ladder_pair(5)
    steps["last", 2]()
    ladder_pair(6)
    ladder_pair(7)

    lane48 = iota((NO, NV), 1)
    odd_half = lane48 // (2 * PART_C) == 1

    def left_block(chunk, carry):
        for half in range(2):
            lower = cut_ref[half, pl.ds(2 * chunk, NO, stride=NO)]
            upper = cut_ref[half, pl.ds(2 * chunk + 1, NO, stride=NO)]
            even_a = jnp.where(odd_half, pltpu.roll(upper, 2 * PART_C, 1), lower)
            odd_a = jnp.where(odd_half, upper, pltpu.roll(lower, 2 * PART_C, 1))
            for odd, piece in enumerate((even_a, odd_a)):
                a = 2 * half + odd
                lanes = pl.ds(pl.multiple_of(chunk * NV, NV), NV)
                left_ref[a * NO : (a + 1) * NO, lanes] = piece.astype(BF16)
                left_ref[(PART_A + a) * NO : (PART_A + a + 1) * NO, lanes] = pltpu.roll(piece, 1, 1).astype(BF16)
        return carry

    lax.fori_loop(0, JP, left_block, 0, unroll=4)

    flat = w_all.reshape(JP * 2 * KC, NV)
    span = 2 * NO
    pltpu.make_async_copy(w_all, w_all, w_sem).wait()

    def cycle_product(n, out):
        right = jnp.concatenate(
            [flat[pl.ds(pl.multiple_of((n * JP_STEP + u) * 2 * KC, 2 * KC), 2 * KC)] for u in range(JP_STEP)], axis=1
        )
        out[...] = jnp.dot(left_ref[...], right, preferred_element_type=F32)

    def cycle_place(n, both):
        for u in range(JP_STEP):
            for odd in range(2):
                j = (n * JP_STEP + u) * 2 + odd
                rows = both[odd * PART_A * NO : (odd + 1) * PART_A * NO, u * NV : (u + 1) * NV]
                got = lanes_at(rows, c_index_ref[occ_s[j]])
                value = got[3 * NO :]
                for a in (2, 1, 0):
                    value = jnp.where(lane48 // SLOTS == a, got[a * NO : (a + 1) * NO], value)
                value = value + 0.5 * ladder_ref[pl.ds(j, NO, stride=NO)]
                start = pl.multiple_of(j * span, NO)
                total_ref[pl.ds(start, NO)] = value
                total_ref[pl.ds(start + NO, NO)] = value

    cycle_product(0, both_a)

    def cycle_pair(n, carry):
        cycle_product(2 * n + 1, both_b)
        cycle_place(2 * n, both_a)
        cycle_product(2 * n + 2, both_a)
        cycle_place(2 * n + 1, both_b)
        return carry

    blocks = JP // JP_STEP
    lax.fori_loop(0, blocks // 2 - 1, cycle_pair, 0)
    cycle_product(blocks - 1, both_b)
    cycle_place(blocks - 2, both_a)
    cycle_place(blocks - 1, both_b)
    total_ref[pl.ds(NO * span, TURN * span)] = total_ref[pl.ds(0, TURN * span)]

    def anti(j, carry):
        ahead = total_ref[pl.ds(j * span + j + 1, TURN, stride=1)]
        across = total_ref[pl.ds((j + 1) * span + j, TURN, stride=span)]
        z_ref[j] = ahead - across
        return carry

    lax.fori_loop(0, NO, anti, 0, unroll=4)
    exchange_part(occ_s, virt8, table, rank, z_ref, own_ref, near_ref, far_ref, *exchange_refs)
    ring.settle()


def contract(occ, virt, virt_row, amplitudes, ladder_pairs, cycle_pairs):
    pairs = NO * NO
    half = (PART_J // 2, TURN, NV)
    vmem = pl.BlockSpec(memory_space=pltpu.VMEM)
    smem = pl.BlockSpec(memory_space=pltpu.SMEM)
    hbm = pl.BlockSpec(memory_space=pl.ANY)
    return pl.pallas_call(
        contract_body,
        out_shape=jax.ShapeDtypeStruct((OUT_ROWS, NV), F32),
        in_specs=[smem, smem, vmem, hbm, hbm, hbm],
        out_specs=vmem,
        scratch_shapes=[
            pltpu.VMEM((ROWS, PART_C, NV), BF16),
            pltpu.VMEM((TILES, 4, ROWS // 8, 16, NV), BF16),
            pltpu.VMEM((JP, KC, 2, NV), BF16),
            pltpu.VMEM((2, PART_C, NV, 2, NV), BF16),
            pltpu.SemaphoreType.DMA,
            pltpu.SemaphoreType.DMA,
            pltpu.SemaphoreType.DMA,
            pltpu.SemaphoreType.DMA,
            pltpu.SemaphoreType.DMA((RING_COPIES + len(PAIRED),)),
            pltpu.VMEM((IRREPS, PART_C, NV), I32),
            pltpu.VMEM((NV, NV), I32),
            pltpu.VMEM((ROWS * 8, NV), F32),
            pltpu.VMEM((2 * IRREPS * SLOTS, 2 * NV), BF16),
            pltpu.VMEM((PART_C, 2, IRREPS, SLOTS, 2 * NV), BF16),
            pltpu.VMEM((IRREPS, 4 * NV, NV), BF16),
            pltpu.VMEM((4, PART_C * SLOTS, 2 * NV), BF16),
            pltpu.VMEM((PART_C * SLOTS, 2 * NV), BF16),
            pltpu.VMEM((pairs, NV), F32),
            pltpu.VMEM((2, pairs, NV), F32),
            pltpu.VMEM((2 * PART_A * NO, 2 * KC), BF16),
            pltpu.VMEM((IRREPS, PART_A * NO, NV), I32),
            pltpu.VMEM(((NO + TURN) * 2 * NO, NV), F32),
            pltpu.VMEM((2 * PART_A * NO, JP_STEP * NV), F32),
            pltpu.VMEM((2 * PART_A * NO, JP_STEP * NV), F32),
            pltpu.VMEM((NO, TURN, NV), F32),
            pltpu.VMEM((2, 3) + half, F32),
            pltpu.VMEM((TILES, SHARE, NV), F32),
            pltpu.VMEM((TILES * PITCH, NV), F32),
            pltpu.VMEM((TILES, SHARE, NV), F32),
            pltpu.VMEM((TILES * PITCH, NV), F32),
            pltpu.VMEM((IRREPS, NV, NV), I32),
            pltpu.VMEM((TILES * PITCH, NV), F32),
            pltpu.VMEM((TILES * PITCH, NV), F32),
            pltpu.SemaphoreType.DMA((2, 3)),
            pltpu.SemaphoreType.DMA((2, 3)),
            pltpu.SemaphoreType.DMA,
            pltpu.SemaphoreType.DMA,
            pltpu.SemaphoreType.DMA,
            pltpu.SemaphoreType.DMA,
            pltpu.SemaphoreType.DMA((2,)),
            pltpu.SemaphoreType.DMA((2,)),
        ],
        compiler_params=pltpu.CompilerParams(
            vmem_limit_bytes=62 * 2**20, collective_id=0, has_side_effects=True
        ),
        name="contract",
    )(occ, virt, virt_row, amplitudes, ladder_pairs, cycle_pairs)


def exchange_part(
    occ_s, virt8, table, rank, z_ref, own_ref, near_ref, far_ref,
    direct_ref, first_ref, first_in, second_ref, second_in,
    index_ref, near_in, far_in, sum_send, sum_recv, a_send, a_recv, b_send, b_recv, f_send, f_recv,
):
    tile = lax.axis_index("tile")
    grp = lax.axis_index("grp")
    up, down, over = (grp + 1) % GRPS, (grp + 3) % GRPS, (grp + 2) % GRPS
    half = PART_J // 2

    def block(owner, part):
        return pl.ds(owner * PART_J + part * half, half)

    def to(axis, target, src, dst, send, recv):
        return pltpu.make_async_remote_copy(
            src_ref=src, dst_ref=dst, send_sem=send, recv_sem=recv,
            device_id={axis: target}, device_id_type=MESH,
        )

    sends = [
        to("grp", peer, z_ref.at[block(peer, part)], direct_ref.at[part, n], sum_send.at[part, n], sum_recv.at[part, n])
        for part in range(2)
        for n, peer in enumerate((over, up, down))
    ]
    for copy in sends:
        copy.start()

    sub = iota((NV, NV), 0)
    lane = iota((NV, NV), 1)
    turned = sub == 4 * (lane % SLOTS) + lane // SLOTS
    rank_turned = spread(rank, turned)[0:1]
    irrep_turned = spread(virt8, turned)[0:1]
    irrep_col = column_of(irrep_turned)
    table_turned = (table % 4) * SLOTS + table // 4
    for irrep in range(IRREPS):
        index_ref[irrep] = pick_rows(table_turned, irrep_col ^ irrep)

    def swap(src, dst, send, recv, target):
        to("tile", target, src.at[target], dst.at[pl.ds(pl.multiple_of(tile * PITCH, PITCH), SHARE)], send, recv).start()

    def swapped(dst, sem):
        rows = dst.at[0 : (TILES - 1) * SHARE]
        pltpu.make_async_copy(rows, rows, sem).wait()

    def first_half(part, value):
        own_ref[part * OWN // 2 : (part + 1) * OWN // 2] = value.reshape(OWN // 2, NV)
        near_tiles = TILES // 2
        for u in range(part * near_tiles, (part + 1) * near_tiles):
            first_ref[u] = own_ref[u * SHARE : (u + 1) * SHARE]
        for d in range(near_tiles):
            target = part * near_tiles + (tile + d) % near_tiles
            if d == 0:
                pl.when(tile // near_tiles != part)(
                    functools.partial(swap, first_ref, first_in, a_send, a_recv, target)
                )
            else:
                swap(first_ref, first_in, a_send, a_recv, target)

    for part in range(2):
        for copy in sends[3 * part : 3 * part + 3]:
            copy.wait_recv()
        first_half(part, z_ref[block(grp, part)] + direct_ref[part, 0] + direct_ref[part, 1] + direct_ref[part, 2])
    first_in[pl.ds(pl.multiple_of(tile * PITCH, PITCH), SHARE)] = first_ref[tile]
    swapped(first_in, a_recv)

    quarter = iota((TILES, NV), 1) // SLOTS

    def one(n, carry):
        row = tile * SHARE + n
        j = grp * PART_J + row // TURN
        i = (j + row % TURN + 1) % NO
        irrep = occ_s[i] ^ occ_s[j]
        rows = first_in[pl.ds(n, TILES, stride=PITCH)]
        full = jnp.concatenate(
            [lanes_at(rows, jnp.broadcast_to(rank_turned + a * SLOTS, (TILES, NV))) for a in range(PART_A)], axis=0
        )
        anti = full - full.T
        got = lanes_at(anti, index_ref[irrep])
        value = got[3 * TILES :]
        for a in (2, 1, 0):
            value = jnp.where(quarter == a, got[a * TILES : (a + 1) * TILES], value)
        for t in range(TILES):
            second_ref[t, pl.ds(n, 1)] = value[t : t + 1]
        return carry

    lax.fori_loop(0, SHARE, one, 0, unroll=3)
    def forward(dst, number, peer):
        for d in range(TILES):
            target = (tile + d) % TILES
            pltpu.make_async_remote_copy(
                src_ref=second_ref.at[target],
                dst_ref=dst.at[pl.ds(pl.multiple_of(tile * PITCH, PITCH), SHARE)],
                send_sem=f_send.at[number], recv_sem=f_recv.at[number],
                device_id={"tile": target, "grp": peer}, device_id_type=MESH,
            ).start()

    def taken(dst, sem, tiles):
        rows = dst.at[0 : tiles * SHARE]
        pltpu.make_async_copy(rows, rows, sem).wait()

    in_near = functools.reduce(lambda one, two: one | two, [tile == u for u in NEAR_TILES])
    in_far = functools.reduce(lambda one, two: one | two, [tile == u for u in FAR_TILES])
    pl.when(in_far)(lambda: forward(far_in, 1, over))
    pl.when(in_near)(lambda: forward(near_in, 0, up))
    for d in range(1, TILES):
        swap(second_ref, second_in, b_send, b_recv, (tile + d) % TILES)
    second_in[pl.ds(pl.multiple_of(tile * PITCH, PITCH), SHARE)] = second_ref[tile]
    swapped(second_in, b_recv)
    for u in range(TILES):
        own_ref[u * SHARE : (u + 1) * SHARE] = second_in[u * PITCH : u * PITCH + SHARE]
    taken(near_in, f_recv.at[0], len(NEAR_TILES))
    for u in NEAR_TILES:
        near_ref[u * SHARE : (u + 1) * SHARE] = near_in[u * PITCH : u * PITCH + SHARE]
    taken(far_in, f_recv.at[1], len(FAR_TILES))
    for u in FAR_TILES:
        far_ref[u * SHARE : (u + 1) * SHARE] = far_in[u * PITCH : u * PITCH + SHARE]
    for copy in sends:
        copy.wait_send()
    swapped(first_in, a_send)
    swapped(second_in, b_send)
    pl.when(in_near)(lambda: taken(near_in, f_send.at[0], TILES))
    pl.when(in_far)(lambda: taken(far_in, f_send.at[1], TILES))


def expand_body(occ_s, virt_ref, in_hbm, out_ref, rows_ref, in_ref, in_sem):
    in_copy = pltpu.make_async_copy(in_hbm, in_ref, in_sem)
    in_copy.start()
    own_ref = in_ref.at[0:OWN]
    near_ref = in_ref.at[OWN : 2 * OWN]
    far_ref = in_ref.at[2 * OWN : 3 * OWN]
    first_a = lax.axis_index("tile") * PART_A
    grp = lax.axis_index("grp")
    first_j = grp * PART_J
    occ_col = occupied_column(occ_s, first_j, NO)
    virt_row = jnp.broadcast_to(virt_ref[...], (NO, NV))
    virt8 = jnp.broadcast_to(virt_ref[...], (8, NV))
    a_irrep = spread(virt8, iota((NV, NV), 0) == first_a + iota((NV, NV), 1) // PART_C)
    in_copy.wait()
    rank_row = jnp.broadcast_to(in_ref[OUT_ROWS - 8 : OUT_ROWS - 7], (NO, NV)).astype(I32)
    n = PART_J
    for x in range(n):
        at = rows_ref.at[x]
        at[x : x + 1] = jnp.zeros((1, NV), F32)
        if x < n - 1:
            at[x + 1 : n] = own_ref[x * TURN : x * TURN + n - 1 - x]
        if x > 0:
            at[0:x] = -own_ref[pl.ds(x - 1, x, stride=TURN - 1)]
        at[n : 2 * n] = own_ref[x * TURN + 11 - x : x * TURN + 23 - x]
        at[2 * n : 2 * n + x + 1] = own_ref[x * TURN + 23 - x : x * TURN + 24]
        if x < n - 1:
            start = (TURN - 1) * (x + 1) + 23 + x
            at[2 * n + x + 1 : 3 * n] = -far_ref[pl.ds(start, n - 1 - x, stride=TURN - 1)]
        at[3 * n : 4 * n] = -near_ref[pl.ds(11 + x, n, stride=TURN - 1)]
    for x in range(n):
        rows = rows_ref[x]
        irrep_j = occ_s[first_j + x]
        for a in range(PART_A):
            got = lanes_at(rows, rank_row + a * SLOTS)
            want = virt_row ^ a_irrep[0:1, a * PART_C : a * PART_C + 1] ^ irrep_j
            value = jnp.where(occ_col == want, got, 0.0)
            for b in range(GRPS):
                start = lax.rem(grp + b, GRPS) * (n * n * PART_A) + x * PART_A + a
                out_ref[pl.ds(start, n, stride=n * PART_A)] = value[b * n : (b + 1) * n]


def expand(occ, virt_row, compact):
    vmem = pl.BlockSpec(memory_space=pltpu.VMEM)
    return pl.pallas_call(
        expand_body,
        out_shape=jax.ShapeDtypeStruct((NO * PART_J * PART_A, NV), F32),
        in_specs=[pl.BlockSpec(memory_space=pltpu.SMEM), vmem, pl.BlockSpec(memory_space=pl.ANY)],
        out_specs=vmem,
        scratch_shapes=[
            pltpu.VMEM((PART_J, NO, NV), F32),
            pltpu.VMEM((OUT_ROWS, NV), F32),
            pltpu.SemaphoreType.DMA,
        ],
        compiler_params=pltpu.CompilerParams(vmem_limit_bytes=62 * 2**20),
        name="expand",
    )(occ, virt_row, compact)


def shards(amplitudes, ladder_ints, cycle_ints, occ_irrep, virt_irrep):
    virt_row = virt_irrep.reshape(1, NV)
    compact = contract(
        occ_irrep, virt_irrep, virt_row, amplitudes,
        ladder_ints.reshape(PART_C, NV, 2, 2, NV), cycle_ints.reshape(KC, JP, 2, NV),
    )
    return expand(occ_irrep, virt_row, compact).reshape(NO, PART_J, PART_A, NV)


def solution(mesh):
    placed = (
        P("tile", "grp", None),
        P("grp", None, "tile", None),
        P(None, "grp", None, None),
        P(),
        P(),
    )
    return jax.shard_map(
        shards, mesh=mesh, in_specs=placed, out_specs=P(None, "grp", "tile", None), check_vma=False
    )
```
